128 devices in a mesh: grid: 32 (over x, z, core), row: 4 (over y).
Axes of the slice: x: 4, y: 4, z: 4, core: 2. Of those that a mesh axis runs over, the one named last changes fastest.
Arguments:
- first_block: bfloat16 [16, 2048, 2048], P('row', 'grid'), may hold values from -6 to 6
- second_block: bfloat16 [16, 2048, 2048], P('row', 'grid'), may hold values from -6 to 6
- spectrum: float32 [2048, 2048], P('grid'), may hold values from 0.07 to 17, as said below
- first_ids: int32 [16], P('row'), may hold values from 0 to 2047
- second_ids: int32 [16], replicated, may hold values from 0 to 2047
- error_scale: float32 [2048], replicated, may hold values from 0.5 to 2
Outputs:
- whitened: float32 [16, 16], P('row')
The draws below stay inside these ranges and needn't reach their ends.
Inputs may be any that keep to these rules, and one draw needn't show every extreme that they name: Every entry is positive, and spectrum[ky, kx] equals spectrum[(2048 - ky) % 2048, (2048 - kx) % 2048].
All inputs are finite; a program needn't handle non-finite values.
Results may differ from the reference program's by a relative error of at most 0.009.
Values may be sent and summed in bfloat16 or wider, within the bound.
No kernel may reach another device: no remote copies, remote signals or barrier semaphores. Data moves between devices by JAX's collectives and lax.ppermute only.
A program may use at most 128 MiB of HBM per device.

```python
import math
import jax
import jax.numpy as jnp
from jax import lax

NX = 2048
NY = 2048
MROWS = 2048
RA = 16
RB = 16


def mirrored(field):
    return jnp.roll(jnp.flip(field, (0, 1)), (1, 1), (0, 1))


def draw_spectrum(key, part):
    key = jax.random.fold_in(key, 11)
    wave_y = jnp.arange(NY, dtype=jnp.float32)
    wave_x = jnp.arange(NX, dtype=jnp.float32)
    freq_y = jnp.minimum(wave_y, NY - wave_y) / NY
    freq_x = jnp.minimum(wave_x, NX - wave_x) / NX
    radius_sq = freq_y[:, None] ** 2 + freq_x[None, :] ** 2
    corr_cells = NX / 16.0
    smooth = (1.0 + (2.0 * math.pi * corr_cells) ** 2 * radius_sq) ** (-1.5)
    rough = jax.random.uniform(key, (NY, NX), jnp.float32, 0.5, 1.5)
    rough = 0.5 * (rough + mirrored(rough))
    return (0.3 + 4.0 * smooth) * rough


def plant(entries, own_key, smallest, top_value):
    dims = entries.shape
    spot = [jax.random.randint(jax.random.fold_in(own_key, axis), (), 0, dims[axis]) for axis in range(len(dims))]
    entries = entries.at[tuple(spot)].set(smallest)
    longest = dims.index(max(dims))
    spot[longest] = (spot[longest] + 1) % dims[longest]
    return entries.at[tuple(spot)].set(top_value)


def levels(own_key, extent, split, low, largest):
    gain, own = 1.0, jax.random.fold_in(own_key, 6)
    for position, parts in split:
        draws = jnp.exp(jax.random.uniform(jax.random.fold_in(own, position), (parts,), jnp.float32, low / len(split), largest / len(split)))
        gain = gain * jnp.repeat(draws, extent[position] // parts).reshape([-1 if axis == position else 1 for axis in range(len(extent))])
    return gain


def scatter_about(own_key, shape, scale, limit, split=(), kind=jnp.bfloat16):
    factor_of = levels(own_key, shape, split, -0.22, 0.18) if split else 1.0
    result = jax.random.normal(own_key, shape, jnp.float32) * scale * factor_of
    return jnp.minimum(jnp.maximum(result, -limit), limit).astype(kind)


def setup_inputs(seed: int = 0) -> dict:
    key_list = jax.random.split(jax.random.key(seed), 7)
    return {
        "first_block": scatter_about(key_list[0], (RA, NX, NY), 1.0, 6.0, ((0, 4), (1, 32))),
        "second_block": scatter_about(key_list[1], (RB, NX, NY), 1.0, 6.0, ((0, 4), (1, 32))),
        "spectrum": draw_spectrum(jax.random.fold_in(key_list[6], 71), 0),
        "first_ids": plant(jax.random.randint(key_list[3], (RA,), 0, MROWS), jax.random.fold_in(key_list[3], 1), 0, MROWS - 1).astype(jnp.int32),
        "second_ids": plant(jax.random.randint(key_list[4], (RB,), 0, MROWS), jax.random.fold_in(key_list[4], 1), 0, MROWS - 1).astype(jnp.int32),
        "error_scale": jnp.clip(jnp.exp(jax.random.uniform(key_list[5], (MROWS,), jnp.float32, math.log(0.5), math.log(2.0))), 0.5, 2.0),
    }


def make_tables(length):
    index_row = jnp.arange(length, dtype=jnp.int32)
    product = (index_row[:, None] * index_row[None, :]) % length
    theta = product.astype(jnp.float32) * (2.0 * math.pi / length)
    return jnp.cos(theta).astype(jnp.bfloat16), jnp.sin(theta).astype(jnp.bfloat16)


def reference(first_block, second_block, spectrum, first_ids, second_ids, error_scale):
    cosine_table, sine_table = make_tables(NX)
    factor = spectrum.T / (NX * NY)

    def mult(left, right):
        return jnp.dot(left, right, preferred_element_type=jnp.float32)

    def apply_prior(sens_row):
        half_real = mult(sens_row, cosine_table).astype(jnp.bfloat16)
        half_imag = (-mult(sens_row, sine_table)).astype(jnp.bfloat16)
        spectral_real = mult(cosine_table, half_real) + mult(sine_table, half_imag)
        spectral_imag = mult(cosine_table, half_imag) - mult(sine_table, half_real)
        scaled_real = (spectral_real * factor).astype(jnp.bfloat16)
        scaled_imag = (spectral_imag * factor).astype(jnp.bfloat16)
        partly_real = (mult(cosine_table, scaled_real) - mult(sine_table, scaled_imag)).astype(jnp.bfloat16)
        partly_imag = (mult(cosine_table, scaled_imag) + mult(sine_table, scaled_real)).astype(jnp.bfloat16)
        return (mult(partly_real, cosine_table) - mult(partly_imag, sine_table)).astype(jnp.bfloat16)

    covaried = lax.map(apply_prior, first_block)
    cross_block = jnp.dot(covaried.reshape(RA, NX * NY), second_block.reshape(RB, NX * NY).T,
                          preferred_element_type=jnp.float32)
    scale_first = error_scale[first_ids]
    scale_second = error_scale[second_ids]
    return cross_block / (NX * scale_first[:, None] * scale_second[None, :])
```

```python
import functools
import math

import jax
import jax.numpy as jnp
import ml_dtypes
import numpy as np
from jax import lax
from jax.experimental import pallas as pl
from jax.experimental.pallas import tpu as pltpu
from jax.sharding import PartitionSpec as P

N = 2048
SLABS = 32
GROUPS = 4
CELLS = N // SLABS
ROWS = 4
WAVES = 8
LANES = ROWS * CELLS
EVERY = ("grid", "row")

NT = (((1,), (1,)), ((), ()))


def rounded(array):
    return np.asarray(array, np.float64).astype(ml_dtypes.bfloat16)


def offsets(kind, j):
    return (4 * j, 4 * j + 2, 8 * (j // 2) + 1 + 6 * (j % 2), 8 * (j // 2) + 5 - 2 * (j % 2))[kind]


@functools.lru_cache(None)
def make_tables():
    y = np.arange(N // 4)
    j = np.arange(WAVES)
    half = np.zeros((4, SLABS // 2, 2, 2, WAVES, N // 4))
    for kind in range(4):
        for low in range(2):
            for slab in range(SLABS // 2):
                waves = CELLS * (slab + SLABS // 2 * (kind // 2)) + 32 * low + offsets(kind, j)
                if kind < 2:
                    angle = 2 * np.pi * ((waves[:, None] * y[None, :]) % N) / N
                    half[kind, slab, low, 0] = np.cos(angle)
                    half[kind, slab, low, 1] = -np.sin(angle)
                    continue
                mirror = waves % 8 != (1 if kind == 2 else 5)
                waves = np.where(mirror, N - waves, waves)
                angle = 2 * np.pi * ((waves[:, None] * y[None, : N // 8]) % N) / N
                sign = np.where(mirror, -1, 1)[:, None]
                half[kind, slab, low, 0] = np.concatenate([np.cos(angle), np.sin(angle)], 1)
                half[kind, slab, low, 1] = sign * np.concatenate([-np.sin(angle), np.cos(angle)], 1)
    half[0, 0, 0, 1, 0] = (-1.0) ** y
    half = rounded(half.reshape(N, N // 4))
    q = np.arange(SLABS)
    angle = 2 * np.pi * ((q[:, None] * q[None, :]) % SLABS) / SLABS
    cos, sin = np.cos(angle), np.sin(angle)
    outer = np.zeros((WAVES, 2, SLABS, SLABS, 2, WAVES))
    for k in range(WAVES):
        outer[k, 0, :, :, 0, k] = cos
        outer[k, 0, :, :, 1, k] = sin
        outer[k, 1, :, :, 1, k] = cos
        outer[k, 1, :, :, 0, k] = -sin
    outer = rounded(outer.reshape(WAVES * 2 * SLABS, -1))
    x = np.arange(CELLS)
    angle = 2 * np.pi * (q[:, None] * x[None, :]) / N
    twist = np.stack([np.tile(np.cos(angle), (1, 2)), np.tile(np.sin(angle), (1, 2))]).astype(np.float32)
    angle = 2 * np.pi * ((x[:, None] * x[None, :]) % CELLS) / CELLS
    cos, sin = np.cos(angle), np.sin(angle)
    inner = np.stack([np.stack([cos, sin], 1), np.stack([-sin, cos], 1)])
    inner = inner.reshape(2, CELLS // 4, 4, 1, 2, 1, CELLS).transpose(0, 2, 3, 1, 4, 5, 6)
    inner = np.broadcast_to(inner, (2, 4, ROWS, CELLS // 4, 2, 2, CELLS))
    inner = rounded(inner.reshape(2 * LANES, LANES))
    return half, outer, twist, inner


PIECES = 4


def half_kernel(a_hbm, b_hbm, table_hbm, out_hbm, block_ref, table_ref, fold_ref, out_ref, block_sem, table_sem, out_sem):
    rows, width = N // PIECES, N // 4
    blocks = [
        pltpu.make_async_copy(hbm, block_ref.at[place], block_sem.at[place]) for place, hbm in enumerate((a_hbm, b_hbm))
    ]
    pieces = [
        pltpu.make_async_copy(
            table_hbm.at[pl.ds(rows * p, rows)], table_ref.at[pl.ds(rows * p, rows)], table_sem.at[p]
        )
        for p in range(PIECES)
    ]
    for copy in blocks + pieces:
        copy.start()
    for place, copy in enumerate(blocks):
        copy.wait()
        own = pl.ds(LANES * place, LANES)
        for side in range(2):
            first, second, third, fourth = (
                block_ref[place, :, pl.ds(width * p + width // 2 * side, width // 2)].astype(jnp.float32)
                for p in range(4)
            )
            even, odd = first + third, second + fourth
            lanes = pl.ds(width // 2 * side, width // 2)
            fold_ref[0, own, lanes] = (even + odd).astype(jnp.bfloat16)
            fold_ref[1, own, lanes] = (even - odd).astype(jnp.bfloat16)
            even, odd = first - third, second - fourth
            if side == 0:
                real, imag = even, -odd
            else:
                turn_real, turn_imag = (even - odd) * math.sqrt(0.5), (even + odd) * -math.sqrt(0.5)
        for kind, sign in ((2, 1.0), (3, -1.0)):
            fold_ref[kind, own, : width // 2] = (real + sign * turn_real).astype(jnp.bfloat16)
            fold_ref[kind, own, width // 2 :] = (imag + sign * turn_imag).astype(jnp.bfloat16)
    sends = []
    for p, copy in enumerate(pieces):
        copy.wait()
        value = lax.dot_general(
            table_ref[pl.ds(rows * p, rows), :], fold_ref[p], NT, preferred_element_type=jnp.float32
        )
        chunks = pl.ds(SLABS // 2 * (p // 2), SLABS // 2), pl.ds(2 * (p % 2), 2)
        out_ref[p] = value.astype(jnp.bfloat16).reshape(SLABS // 2, 2, 16, 2 * LANES)
        send = pltpu.make_async_copy(out_ref.at[p], out_hbm.at[chunks], out_sem.at[p])
        send.start()
        sends.append(send)
    for send in sends:
        send.wait()


def half_transform(first, second, table):
    return pl.pallas_call(
        half_kernel,
        in_specs=[pl.BlockSpec(memory_space=pl.ANY)] * 3,
        out_specs=pl.BlockSpec(memory_space=pl.ANY),
        out_shape=jax.ShapeDtypeStruct((SLABS, GROUPS, 16, 2 * LANES), jnp.bfloat16),
        scratch_shapes=[
            pltpu.VMEM((2, LANES, N), jnp.bfloat16),
            pltpu.VMEM((N, N // 4), jnp.bfloat16),
            pltpu.VMEM((4, 2 * LANES, N // 4), jnp.bfloat16),
            pltpu.VMEM((PIECES, SLABS // 2, 2, 16, 2 * LANES), jnp.bfloat16),
            pltpu.SemaphoreType.DMA((2,)),
            pltpu.SemaphoreType.DMA((PIECES,)),
            pltpu.SemaphoreType.DMA((PIECES,)),
        ],
        compiler_params=pltpu.CompilerParams(vmem_limit_bytes=60 * 2**20),
        cost_estimate=pl.CostEstimate(flops=N * 1024 * 512, bytes_accessed=6 * 2**20, transcendentals=0),
    )(first, second, table)


def turned(value, amount):
    amount = (SLABS * amount) % 128
    return pltpu.roll(value, amount, 1) if amount else value


def weight_kernel(spectrum_ref, nyquist_ref, weight_ref, shift_ref):
    slab, group = lax.axis_index("grid"), lax.axis_index("row")
    own = spectrum_ref[pl.ds(pl.multiple_of(32 * (group % 2), 32), 32), :]
    own = jnp.concatenate([own, jnp.broadcast_to(nyquist_ref[...], (8, N))], axis=0)
    own = jnp.concatenate([own[:, 128 * c : 128 * (c + 1)] for c in range(16)], axis=0)
    kind = 2 * (slab // (SLABS // 2)) + group // 2
    shape = ((WAVES + 1) * 16, 16 * 40)
    below, along = lax.broadcasted_iota(jnp.int32, (shape[0], 1), 0), lax.broadcasted_iota(jnp.int32, shape, 1)
    wave, coarse = below // 16, below % 16
    wanted = jnp.zeros_like(wave)
    for each in range(4):
        wanted = jnp.where(kind == each, offsets(each, wave), wanted)
    wanted = coarse * 40 + jnp.where(wave < WAVES, wanted, 32)
    pick = jnp.where(along == wanted, 1.0, 0.0).astype(jnp.bfloat16)
    spread = jnp.zeros((shape[0], 128), jnp.float32)
    for _ in range(3):
        piece = own.astype(jnp.bfloat16)
        own = own - piece.astype(jnp.float32)
        spread += jnp.dot(pick, piece, preferred_element_type=jnp.float32)
    alone = jnp.where((slab == 0) & (group == 0), 1.0, 0.0)
    shift_ref[...] = (spread[16 * WAVES :] - spread[:16]) * (alone / N**2)
    columns = [
        spread[16 * wave : 16 * (wave + 1)] * ((2.0 - alone) / N**2 if wave == 0 else 2.0 / N**2)
        for wave in range(WAVES)
    ]
    quarter = lax.broadcasted_iota(jnp.int32, (16, 128), 1) // SLABS
    for fine in range(4):
        for half in range(2):
            weight = jnp.zeros((16, 128), jnp.float32)
            for place in range(4):
                weight = jnp.where(quarter == place, turned(columns[4 * half + place], place - fine), weight)
            weight_ref[fine, :, 128 * half : 128 * (half + 1)] = weight


def spectrum_weights(spectrum, nyquist):
    return pl.pallas_call(
        weight_kernel,
        in_specs=[pl.BlockSpec(memory_space=pltpu.VMEM)] * 2,
        out_specs=[pl.BlockSpec(memory_space=pltpu.VMEM)] * 2,
        out_shape=[
            jax.ShapeDtypeStruct((4, 16, LANES), jnp.float32),
            jax.ShapeDtypeStruct((16, 128), jnp.float32),
        ],
        compiler_params=pltpu.CompilerParams(vmem_limit_bytes=16 * 2**20),
        cost_estimate=pl.CostEstimate(flops=10**9, bytes_accessed=2**20, transcendentals=0),
    )(spectrum, nyquist)


def cross_kernel(x_ref, outer_ref, twist_ref, inner_ref, weight_ref, shift_ref, out_ref, za_ref, zb_ref, ze_ref, a_ref, b_ref):
    wide = jnp.float32
    cos, sin = (jnp.concatenate([twist_ref[k], twist_ref[k]], axis=1) for k in range(2))

    def twisted(real, imag):
        return (real * cos + imag * sin).astype(jnp.bfloat16), (imag * cos - real * sin).astype(jnp.bfloat16)

    along = lax.broadcasted_iota(jnp.int32, (2 * SLABS, SLABS * 16), 1) % 16
    extra = jnp.where(along == WAVES, outer_ref[: 2 * SLABS], 0.0).astype(jnp.bfloat16)

    for group in range(GROUPS):
        cells = x_ref[:, group].reshape(SLABS * 16, 2 * LANES)
        mixed = jnp.dot(outer_ref[...], cells, preferred_element_type=wide)
        for wave in range(WAVES):
            rows = pl.ds(SLABS * wave, SLABS)
            for place, ref in enumerate((za_ref, zb_ref)):
                lanes = slice(place * LANES, (place + 1) * LANES)
                first = 2 * SLABS * wave
                real, imag = mixed[first : first + SLABS, lanes], mixed[first + SLABS : first + 2 * SLABS, lanes]
                ref[group, rows, :LANES], ref[group, rows, LANES:] = twisted(real, imag)
        mixed = jnp.dot(extra, cells[:, :LANES], preferred_element_type=wide)
        rows = pl.ds(SLABS * group, SLABS)
        ze_ref[rows, :LANES], ze_ref[rows, LANES:] = twisted(mixed[:SLABS], mixed[SLABS:])

    quarter = lax.broadcasted_iota(jnp.int32, (16, 128), 1) // SLABS
    changes = [jnp.where(quarter == 0, turned(shift_ref[...], -fine), 0.0) for fine in range(4)]
    changes = [jnp.concatenate([change] * ROWS, axis=0) for change in changes]
    weights = [jnp.concatenate([weight_ref[fine]] * ROWS, axis=0) for fine in range(4)]
    below = lax.broadcasted_iota(jnp.int32, (2 * LANES, 128), 0) // 16 % ROWS
    along = lax.broadcasted_iota(jnp.int32, (2 * LANES, 128), 1) // CELLS
    inner = jnp.concatenate(
        [
            jnp.where(below == along + 2 * pair, inner_ref[:, 128 * part : 128 * (part + 1)], 0.0).astype(jnp.bfloat16)
            for part in range(2)
            for pair in range(2)
        ],
        axis=1,
    )
    apart = lax.dot_general(inner, ze_ref[...], NT, preferred_element_type=wide)
    for group in range(GROUPS):
        own = pl.ds(64 * group, 64)
        value = lax.dot_general(inner, za_ref[group], NT, preferred_element_type=wide)
        moved = turned(apart, -group)
        for part in range(2):
            for fine in range(4):
                rows = slice(LANES * part + 64 * fine, LANES * part + 64 * (fine + 1))
                scaled = value[rows] * weights[fine]
                a_ref[part, fine, own, :128] = (scaled[:, :128] + moved[rows] * changes[fine]).astype(jnp.bfloat16)
                a_ref[part, fine, own, 128:] = scaled[:, 128:].astype(jnp.bfloat16)
        value = lax.dot_general(inner, zb_ref[group], NT, preferred_element_type=wide)
        for part in range(2):
            for fine in range(4):
                rows = slice(LANES * part + 64 * fine, LANES * part + 64 * (fine + 1))
                b_ref[part, fine, own] = value[rows].astype(jnp.bfloat16)

    product = jnp.zeros((LANES, LANES), wide)
    for part in range(2):
        for fine in range(4):
            product += lax.dot_general(a_ref[part, fine], b_ref[part, fine], NT, preferred_element_type=wide)
    below = lax.broadcasted_iota(jnp.int32, (LANES, LANES), 0)
    along = lax.broadcasted_iota(jnp.int32, (LANES, LANES), 1)
    product = jnp.where(below % 16 == along % 16, product, 0.0)
    rows = [product[16 * k : 16 * (k + 1)].sum(0, keepdims=True) for k in range(16)]
    rows = jnp.concatenate(rows, axis=0)
    lane = lax.broadcasted_iota(jnp.int32, (16, 128), 1) % 16
    below = lax.broadcasted_iota(jnp.int32, (16, 128), 0) % ROWS
    total = jnp.zeros((16, 128), wide)
    for half in range(2):
        value = rows[:, 128 * half : 128 * (half + 1)]
        for shift in (8, 4, 2, 1):
            near, far = pltpu.roll(value, 128 - shift, 1), pltpu.roll(value, 16 - shift, 1)
            value = value + jnp.where(lane < 16 - shift, near, far)
        total += jnp.where(lane == ROWS * half + below, value, 0.0)
    sums = [total[ROWS * group : ROWS * (group + 1)].sum(0, keepdims=True) for group in range(GROUPS)]
    for slab in range(SLABS):
        for group in range(GROUPS):
            out_ref[slab * GROUPS + group] = sums[group]


def cross_partial(arrived, outer, twist, inner, weight, shift):
    return pl.pallas_call(
        cross_kernel,
        in_specs=[pl.BlockSpec(memory_space=pltpu.VMEM)] * 6,
        out_specs=pl.BlockSpec(memory_space=pltpu.VMEM),
        out_shape=jax.ShapeDtypeStruct((SLABS * GROUPS, 1, 128), jnp.float32),
        scratch_shapes=[
            pltpu.VMEM((GROUPS, LANES, 2 * LANES), jnp.bfloat16),
            pltpu.VMEM((GROUPS, LANES, 2 * LANES), jnp.bfloat16),
            pltpu.VMEM((128, 2 * LANES), jnp.bfloat16),
            pltpu.VMEM((2, 4, LANES, LANES), jnp.bfloat16),
            pltpu.VMEM((2, 4, LANES, LANES), jnp.bfloat16),
        ],
        compiler_params=pltpu.CompilerParams(vmem_limit_bytes=36 * 2**20),
        cost_estimate=pl.CostEstimate(flops=3 * 10**9, bytes_accessed=5 * 2**20, transcendentals=0),
    )(arrived, outer, twist, inner, weight, shift)


def lookup(indices, table):
    onehot = indices[:, None] == jnp.arange(table.shape[0], dtype=jnp.int32)[None, :]
    return jnp.sum(jnp.where(onehot, table[None, :], 0.0), axis=1)


def shards(first_block, second_block, spectrum, first_ids, second_ids, error_scale):
    half, outer, twist, inner = (jnp.asarray(t) for t in make_tables())
    sent = half_transform(first_block.reshape(LANES, N), second_block.reshape(LANES, N), half)
    sent = sent.reshape(SLABS * GROUPS, 16, 2 * LANES)
    arrived = lax.all_to_all(sent, EVERY, 0, 0, tiled=True)
    nyquist = lax.ppermute(spectrum[:1], "grid", [(SLABS // 2, 0)])
    weight, shift = spectrum_weights(spectrum, nyquist)
    arrived = arrived.reshape(SLABS, GROUPS, 16, 2 * LANES)
    partial = cross_partial(arrived, outer, twist, inner, weight, shift)
    partial = lax.all_to_all(partial, EVERY, 0, 0, tiled=True)
    cross = partial.sum((0, 1)).reshape(2, ROWS, 2, 2, ROWS)[:, :, 0]
    cross = cross.transpose(3, 2, 0, 1).reshape(ROWS, GROUPS * ROWS)
    scale_first = lookup(first_ids, error_scale)
    scale_second = lookup(second_ids, error_scale)
    return cross / (N * scale_first[:, None] * scale_second[None, :])


def solution(mesh):
    return jax.shard_map(
        shards,
        mesh=mesh,
        in_specs=(
            P("row", "grid", None),
            P("row", "grid", None),
            P("grid", None),
            P("row"),
            P(),
            P(),
        ),
        out_specs=P("row", None),
        check_vma=False,
    )
```

```python
import functools
import math

import jax
import jax.numpy as jnp
import ml_dtypes
import numpy as np
from jax import lax
from jax.experimental import pallas as pl
from jax.experimental.pallas import tpu as pltpu
from jax.sharding import PartitionSpec as P

N = 2048
SLABS = 32
GROUPS = 4
CELLS = N // SLABS
ROWS = 4
WAVES = 8
KINDS = 8
LANES = ROWS * CELLS
EVERY = ("grid", "row")

NT = (((1,), (1,)), ((), ()))


def rounded(array):
    return np.asarray(array, np.float64).astype(ml_dtypes.bfloat16)


BASES = (0, 4, 2, 10, 1, 9, 5, 13)


def offsets(kind, j):
    if kind < 2:
        return 8 * j + BASES[kind]
    return 16 * (j // 2) + BASES[kind] + (16 - 2 * BASES[kind]) * (j % 2)


@functools.lru_cache(None)
def make_tables():
    y = np.arange(N // 8)
    j = np.arange(WAVES)
    half = np.zeros((KINDS, SLABS // 2, 2, WAVES, N // 8))
    for kind in range(KINDS):
        for slab in range(SLABS // 2):
            waves = CELLS * (slab + SLABS // 2 * (kind // 4)) + offsets(kind, j)
            if kind < 2:
                angle = 2 * np.pi * ((waves[:, None] * y[None, :]) % N) / N
                half[kind, slab, 0] = np.cos(angle)
                half[kind, slab, 1] = -np.sin(angle)
                continue
            mirror = waves % 16 != BASES[kind]
            waves = np.where(mirror, N - waves, waves)
            angle = 2 * np.pi * ((waves[:, None] * y[None, : N // 16]) % N) / N
            sign = np.where(mirror, -1, 1)[:, None]
            half[kind, slab, 0] = np.concatenate([np.cos(angle), np.sin(angle)], 1)
            half[kind, slab, 1] = sign * np.concatenate([-np.sin(angle), np.cos(angle)], 1)
    half[0, 0, 1, 0] = (-1.0) ** y
    half = rounded(half.reshape(N, N // 8))
    q = np.arange(SLABS).reshape(SLABS // 2, 2).T.reshape(SLABS)
    angle = 2 * np.pi * ((q[:, None] * np.arange(SLABS // 2)[None, :]) % SLABS) / SLABS
    cos, sin = np.cos(angle).reshape(2, SLABS // 2, -1), np.sin(angle).reshape(2, SLABS // 2, -1)
    outer = np.zeros((2, WAVES, 2, SLABS // 2, SLABS // 2, 2, WAVES))
    for k in range(WAVES):
        outer[:, k, 0, :, :, 0, k] = cos
        outer[:, k, 0, :, :, 1, k] = sin
        outer[:, k, 1, :, :, 1, k] = cos
        outer[:, k, 1, :, :, 0, k] = -sin
    outer = rounded(outer.reshape(2, LANES, LANES))
    x = np.arange(CELLS)
    angle = 2 * np.pi * (q[:, None] * x[None, :]) / N
    twist = np.stack([np.tile(np.cos(angle), (1, 2)), np.tile(np.sin(angle), (1, 2))]).astype(np.float32)
    angle = 2 * np.pi * ((x[:, None] * x[None, :]) % CELLS) / CELLS
    cos, sin = np.cos(angle), np.sin(angle)
    inner = np.stack([np.stack([cos, sin], 1), np.stack([-sin, cos], 1)])
    inner = inner.reshape(2, CELLS // 4, 4, 1, 2, 1, CELLS).transpose(0, 2, 3, 1, 4, 5, 6)
    inner = np.broadcast_to(inner, (2, 4, ROWS, CELLS // 4, 2, 2, CELLS))
    inner = rounded(inner.reshape(2 * LANES, LANES))
    return half, outer, twist, inner


SPLIT = 4


def fold(parts):
    even = [parts[k] + parts[k + 8] for k in range(8)]
    odd = [parts[k] - parts[k + 8] for k in range(8)]
    both = [even[k] + even[k + 4] for k in range(4)]
    less = [even[k] - even[k + 4] for k in range(4)]
    yield both[0] + both[2], both[1] + both[3]
    yield both[0] - both[2], both[1] - both[3]
    half = math.sqrt(0.5)
    pairs = [((less[0], -less[2]), (less[1], -less[3]), math.pi / 4)]
    near = [(odd[k], -odd[k + 4]) for k in range(2)]
    far = [(half * (odd[k + 2] - odd[k + 6]), -half * (odd[k + 2] + odd[k + 6])) for k in range(2)]
    pairs.append(tuple((near[k][0] + far[k][0], near[k][1] + far[k][1]) for k in range(2)) + (math.pi / 8,))
    pairs.append(tuple((near[k][0] - far[k][0], near[k][1] - far[k][1]) for k in range(2)) + (5 * math.pi / 8,))
    for (real, imag), (next_real, next_imag), angle in pairs:
        cos, sin = math.cos(angle), math.sin(angle)
        turn_real, turn_imag = cos * next_real + sin * next_imag, cos * next_imag - sin * next_real
        yield real + turn_real, imag + turn_imag
        yield real - turn_real, imag - turn_imag


def half_kernel(a_hbm, b_hbm, table_hbm, out_hbm, block_ref, table_ref, fold_ref, out_ref, block_sem, table_sem, out_sem):
    rows = LANES // SPLIT
    blocks = [
        [
            pltpu.make_async_copy(
                hbm.at[pl.ds(rows * k, rows)], block_ref.at[place, pl.ds(rows * k, rows)], block_sem.at[place, k]
            )
            for k in range(SPLIT)
        ]
        for place, hbm in enumerate((a_hbm, b_hbm))
    ]
    tables = [
        pltpu.make_async_copy(
            table_hbm.at[pl.ds(N // 2 * k, N // 2)], table_ref.at[pl.ds(N // 2 * k, N // 2)], table_sem.at[k]
        )
        for k in range(2)
    ]
    for copy in blocks[0] + tables[:1] + blocks[1] + tables[1:]:
        copy.start()

    for place in range(2):
        for k in range(SPLIT):
            blocks[place][k].wait()

            def fold_rows(step, carry):
                row = pl.multiple_of(rows * k + 16 * step, 16)
                parts = [block_ref[place, pl.ds(row, 16), pl.ds(128 * p, 128)].astype(jnp.float32) for p in range(16)]
                own = pl.ds(pl.multiple_of(LANES * place + row, 16), 16)
                for kind, (first, second) in enumerate(fold(parts)):
                    fold_ref[kind, own, :128] = first.astype(jnp.bfloat16)
                    fold_ref[kind, own, 128:] = second.astype(jnp.bfloat16)
                return carry

            lax.fori_loop(0, rows // 16, fold_rows, 0, unroll=True)
    sends = []
    for kind in range(KINDS):
        if kind % 4 == 0:
            tables[kind // 4].wait()
        value = lax.dot_general(
            table_ref[pl.ds(LANES * kind, LANES), :], fold_ref[kind], NT, preferred_element_type=jnp.float32
        )
        out_ref[kind] = value.astype(jnp.bfloat16).reshape(SLABS // 2, 16, 2 * LANES)
        send = pltpu.make_async_copy(
            out_ref.at[kind], out_hbm.at[pl.ds(SLABS // 2 * (kind // 4), SLABS // 2), kind % 4], out_sem.at[kind]
        )
        send.start()
        sends.append(send)
    for send in sends:
        send.wait()


def half_transform(first, second, table):
    return pl.pallas_call(
        half_kernel,
        in_specs=[pl.BlockSpec(memory_space=pl.ANY)] * 3,
        out_specs=pl.BlockSpec(memory_space=pl.ANY),
        out_shape=jax.ShapeDtypeStruct((SLABS, GROUPS, 16, 2 * LANES), jnp.bfloat16),
        scratch_shapes=[
            pltpu.VMEM((2, LANES, N), jnp.bfloat16),
            pltpu.VMEM((N, N // 8), jnp.bfloat16),
            pltpu.VMEM((KINDS, 2 * LANES, N // 8), jnp.bfloat16),
            pltpu.VMEM((KINDS, SLABS // 2, 16, 2 * LANES), jnp.bfloat16),
            pltpu.SemaphoreType.DMA((2, SPLIT)),
            pltpu.SemaphoreType.DMA((2,)),
            pltpu.SemaphoreType.DMA((KINDS,)),
        ],
        compiler_params=pltpu.CompilerParams(vmem_limit_bytes=60 * 2**20),
        cost_estimate=pl.CostEstimate(flops=N * 512 * 512, bytes_accessed=5 * 2**20, transcendentals=0),
    )(first, second, table)


def turned(value, amount):
    amount = (SLABS * amount) % 128
    return pltpu.roll(value, amount, 1) if amount else value


def weight_kernel(spectrum_ref, nyquist_ref, weight_ref, shift_ref):
    slab, group = lax.axis_index("grid"), lax.axis_index("row")
    own = jnp.concatenate([spectrum_ref[...], jnp.broadcast_to(nyquist_ref[...], (8, N))], axis=0)
    own = jnp.concatenate([own[:, 128 * c : 128 * (c + 1)] for c in range(16)], axis=0)
    mine = 4 * (slab // (SLABS // 2)) + group
    height = CELLS + 8
    shape = ((WAVES + 1) * 16, 16 * height)
    below, along = lax.broadcasted_iota(jnp.int32, (shape[0], 1), 0), lax.broadcasted_iota(jnp.int32, shape, 1)
    wave, coarse = below // 16, below % 16
    wanted = jnp.zeros_like(wave)
    for kind in range(KINDS):
        wanted = jnp.where(mine == kind, offsets(kind, wave), wanted)
    wanted = coarse * height + jnp.where(wave < WAVES, wanted, CELLS)
    pick = jnp.where(along == wanted, 1.0, 0.0).astype(jnp.bfloat16)
    below, along = (lax.broadcasted_iota(jnp.int32, (128, 128), axis) for axis in range(2))
    moved = along // SLABS * SLABS + 2 * (along % 16) + along % SLABS // 16
    order = jnp.where(below == moved, 1.0, 0.0).astype(jnp.bfloat16)
    spread = jnp.zeros((shape[0], 128), jnp.float32)
    for _ in range(3):
        piece = own.astype(jnp.bfloat16)
        own = own - piece.astype(jnp.float32)
        picked = jnp.dot(pick, piece, preferred_element_type=jnp.float32).astype(jnp.bfloat16)
        spread += jnp.dot(picked, order, preferred_element_type=jnp.float32)
    alone = jnp.where((slab == 0) & (group == 0), 1.0, 0.0)
    shift_ref[...] = (spread[16 * WAVES :] - spread[:16]) * (alone / N**2)
    columns = [
        spread[16 * wave : 16 * (wave + 1)] * ((2.0 - alone) / N**2 if wave == 0 else 2.0 / N**2)
        for wave in range(WAVES)
    ]
    quarter = lax.broadcasted_iota(jnp.int32, (16, 128), 1) // SLABS
    for fine in range(4):
        for half in range(2):
            weight = jnp.zeros((16, 128), jnp.float32)
            for place in range(4):
                weight = jnp.where(quarter == place, turned(columns[4 * half + place], place - fine), weight)
            weight_ref[fine, :, 128 * half : 128 * (half + 1)] = weight


def spectrum_weights(spectrum, nyquist):
    return pl.pallas_call(
        weight_kernel,
        in_specs=[pl.BlockSpec(memory_space=pltpu.VMEM)] * 2,
        out_specs=[pl.BlockSpec(memory_space=pltpu.VMEM)] * 2,
        out_shape=[
            jax.ShapeDtypeStruct((4, 16, LANES), jnp.float32),
            jax.ShapeDtypeStruct((16, 128), jnp.float32),
        ],
        compiler_params=pltpu.CompilerParams(vmem_limit_bytes=16 * 2**20),
        cost_estimate=pl.CostEstimate(flops=10**9, bytes_accessed=2**20, transcendentals=0),
    )(spectrum, nyquist)


def cross_kernel(x_ref, outer_ref, twist_ref, inner_ref, weight_ref, shift_ref, out_ref, za_ref, zb_ref, ze_ref, a_ref, b_ref):
    wide = jnp.float32
    cosines, sines = (jnp.concatenate([twist_ref[k], twist_ref[k]], axis=1) for k in range(2))

    nine = lax.broadcasted_iota(jnp.int32, (SLABS, LANES), 1) % 16 == WAVES
    for group in range(GROUPS):
        low, high = x_ref[: SLABS // 2, group], x_ref[SLABS // 2 :, group]
        for odd, cells in enumerate((low + high, low - high)):
            cells = cells.reshape(LANES, 2 * LANES)
            outer = outer_ref[odd]
            mixed = jnp.dot(outer, cells, preferred_element_type=wide)
            step = SLABS // 2
            cos, sin = cosines[step * odd : step * (odd + 1)], sines[step * odd : step * (odd + 1)]

            def twisted(real, imag):
                return (real * cos + imag * sin).astype(jnp.bfloat16), (imag * cos - real * sin).astype(jnp.bfloat16)

            for wave in range(WAVES):
                rows = pl.ds(SLABS * wave + step * odd, step)
                for place, ref in enumerate((za_ref, zb_ref)):
                    lanes = slice(place * LANES, (place + 1) * LANES)
                    first = 2 * step * wave
                    real, imag = mixed[first : first + step, lanes], mixed[first + step : first + 2 * step, lanes]
                    ref[group, rows, :LANES], ref[group, rows, LANES:] = twisted(real, imag)
            extra = jnp.where(nine, outer[:SLABS], 0.0).astype(jnp.bfloat16)
            mixed = jnp.dot(extra, cells[:, :LANES], preferred_element_type=wide)
            rows = pl.ds(SLABS * group + step * odd, step)
            ze_ref[rows, :LANES], ze_ref[rows, LANES:] = twisted(mixed[:step], mixed[step:])

    quarter = lax.broadcasted_iota(jnp.int32, (16, 128), 1) // SLABS
    changes = [jnp.where(quarter == 0, turned(shift_ref[...], -fine), 0.0) for fine in range(4)]
    changes = [jnp.concatenate([change] * ROWS, axis=0) for change in changes]
    weights = [jnp.concatenate([weight_ref[fine]] * ROWS, axis=0) for fine in range(4)]
    below = lax.broadcasted_iota(jnp.int32, (2 * LANES, 128), 0) // 16 % ROWS
    along = lax.broadcasted_iota(jnp.int32, (2 * LANES, 128), 1) // CELLS
    inner = jnp.concatenate(
        [
            jnp.where(below == along + 2 * pair, inner_ref[:, 128 * part : 128 * (part + 1)], 0.0).astype(jnp.bfloat16)
            for part in range(2)
            for pair in range(2)
        ],
        axis=1,
    )
    apart = lax.dot_general(inner, ze_ref[...], NT, preferred_element_type=wide)
    for group in range(GROUPS):
        own = pl.ds(64 * group, 64)
        value = lax.dot_general(inner, za_ref[group], NT, preferred_element_type=wide)
        moved = turned(apart, -group)
        for part in range(2):
            for fine in range(4):
                rows = slice(LANES * part + 64 * fine, LANES * part + 64 * (fine + 1))
                scaled = value[rows] * weights[fine]
                a_ref[part, fine, own, :128] = (scaled[:, :128] + moved[rows] * changes[fine]).astype(jnp.bfloat16)
                a_ref[part, fine, own, 128:] = scaled[:, 128:].astype(jnp.bfloat16)
        value = lax.dot_general(inner, zb_ref[group], NT, preferred_element_type=wide)
        for part in range(2):
            for fine in range(4):
                rows = slice(LANES * part + 64 * fine, LANES * part + 64 * (fine + 1))
                b_ref[part, fine, own] = value[rows].astype(jnp.bfloat16)

    product = jnp.zeros((LANES, LANES), wide)
    for part in range(2):
        for fine in range(4):
            product += lax.dot_general(a_ref[part, fine], b_ref[part, fine], NT, preferred_element_type=wide)
    below = lax.broadcasted_iota(jnp.int32, (LANES, LANES), 0)
    along = lax.broadcasted_iota(jnp.int32, (LANES, LANES), 1)
    product = jnp.where(below % 16 == along % 16, product, 0.0)
    rows = jnp.concatenate([product[16 * k : 16 * (k + 1)].sum(0, keepdims=True) for k in range(16)], axis=0)
    below, along = (lax.broadcasted_iota(jnp.int32, (LANES, 128), axis) for axis in range(2))
    gather = jnp.where(below // 16 == along % 16, 1.0, 0.0).astype(jnp.bfloat16)
    total = jnp.zeros((16, 128), wide)
    for _ in range(3):
        piece = rows.astype(jnp.bfloat16)
        rows = rows - piece.astype(wide)
        total += jnp.dot(piece, gather, preferred_element_type=wide)
    below, along = (lax.broadcasted_iota(jnp.int32, (16, 128), axis) for axis in range(2))
    total = jnp.where(below % ROWS == along // 16, total, 0.0)
    sums = [total[ROWS * group : ROWS * (group + 1)].sum(0, keepdims=True) for group in range(GROUPS)]
    for slab in range(SLABS):
        for group in range(GROUPS):
            out_ref[slab * GROUPS + group] = sums[group]


def cross_partial(arrived, outer, twist, inner, weight, shift):
    return pl.pallas_call(
        cross_kernel,
        in_specs=[pl.BlockSpec(memory_space=pltpu.VMEM)] * 6,
        out_specs=pl.BlockSpec(memory_space=pltpu.VMEM),
        out_shape=jax.ShapeDtypeStruct((SLABS * GROUPS, 1, 128), jnp.float32),
        scratch_shapes=[
            pltpu.VMEM((GROUPS, LANES, 2 * LANES), jnp.bfloat16),
            pltpu.VMEM((GROUPS, LANES, 2 * LANES), jnp.bfloat16),
            pltpu.VMEM((128, 2 * LANES), jnp.bfloat16),
            pltpu.VMEM((2, 4, LANES, LANES), jnp.bfloat16),
            pltpu.VMEM((2, 4, LANES, LANES), jnp.bfloat16),
        ],
        compiler_params=pltpu.CompilerParams(vmem_limit_bytes=36 * 2**20),
        cost_estimate=pl.CostEstimate(flops=3 * 10**9, bytes_accessed=5 * 2**20, transcendentals=0),
    )(arrived, outer, twist, inner, weight, shift)


def lookup(indices, table):
    onehot = indices[:, None] == jnp.arange(table.shape[0], dtype=jnp.int32)[None, :]
    return jnp.sum(jnp.where(onehot, table[None, :], 0.0), axis=1)


def shards(first_block, second_block, spectrum, first_ids, second_ids, error_scale):
    half, outer, twist, inner = (jnp.asarray(t) for t in make_tables())
    sent = half_transform(first_block.reshape(LANES, N), second_block.reshape(LANES, N), half)
    sent = sent.reshape(SLABS * GROUPS, 16, 2 * LANES)
    arrived = lax.all_to_all(sent, EVERY, 0, 0, tiled=True)
    nyquist = lax.ppermute(spectrum[:1], "grid", [(SLABS // 2, 0)])
    weight, shift = spectrum_weights(spectrum, nyquist)
    arrived = arrived.reshape(SLABS, GROUPS, 16, 2 * LANES)
    partial = cross_partial(arrived, outer, twist, inner, weight, shift)
    partial = lax.all_to_all(partial, EVERY, 0, 0, tiled=True)
    cross = partial.sum((0, 1))[:64].reshape(ROWS, GROUPS * ROWS)
    scale_first = lookup(first_ids, error_scale)
    scale_second = lookup(second_ids, error_scale)
    return cross / (N * scale_first[:, None] * scale_second[None, :])


def solution(mesh):
    return jax.shard_map(
        shards,
        mesh=mesh,
        in_specs=(
            P("row", "grid", None),
            P("row", "grid", None),
            P("grid", None),
            P("row"),
            P(),
            P(),
        ),
        out_specs=P("row", None),
        check_vma=False,
    )
```

```python
import functools
import math

import jax
import jax.numpy as jnp
import ml_dtypes
import numpy as np
from jax import lax
from jax.experimental import pallas as pl
from jax.experimental.pallas import tpu as pltpu
from jax.sharding import PartitionSpec as P

N = 2048
SLABS = 32
GROUPS = 4
CELLS = N // SLABS
ROWS = 4
WAVES = 8
KINDS = 8
LANES = ROWS * CELLS
EVERY = ("grid", "row")

NT = (((1,), (1,)), ((), ()))


def rounded(array):
    return np.asarray(array, np.float64).astype(ml_dtypes.bfloat16)


BASES = (0, 4, 2, 10, 1, 9, 5, 13)


def offsets(kind, j):
    if kind < 2:
        return 8 * j + BASES[kind]
    return 16 * (j // 2) + BASES[kind] + (16 - 2 * BASES[kind]) * (j % 2)


@functools.lru_cache(None)
def make_tables():
    y = np.arange(N // 8)
    j = np.arange(WAVES)
    half = np.zeros((KINDS, SLABS // 2, 2, WAVES, N // 8))
    for kind in range(KINDS):
        for slab in range(SLABS // 2):
            waves = CELLS * (slab + SLABS // 2 * (kind // 4)) + offsets(kind, j)
            if kind < 2:
                angle = 2 * np.pi * ((waves[:, None] * y[None, :]) % N) / N
                half[kind, slab, 0] = np.cos(angle)
                half[kind, slab, 1] = -np.sin(angle)
                continue
            mirror = waves % 16 != BASES[kind]
            waves = np.where(mirror, N - waves, waves)
            angle = 2 * np.pi * ((waves[:, None] * y[None, : N // 16]) % N) / N
            sign = np.where(mirror, -1, 1)[:, None]
            half[kind, slab, 0] = np.concatenate([np.cos(angle), np.sin(angle)], 1)
            half[kind, slab, 1] = sign * np.concatenate([-np.sin(angle), np.cos(angle)], 1)
    half[0, 0, 1, 0] = (-1.0) ** y
    half = rounded(half.reshape(N, N // 8))
    q = np.arange(SLABS).reshape(SLABS // 2, 2).T.reshape(SLABS)
    angle = 2 * np.pi * ((q[:, None] * np.arange(SLABS // 2)[None, :]) % SLABS) / SLABS
    cos, sin = np.cos(angle).reshape(2, SLABS // 2, -1), np.sin(angle).reshape(2, SLABS // 2, -1)
    outer = np.zeros((2, WAVES, 2, SLABS // 2, SLABS // 2, 2, WAVES))
    for k in range(WAVES):
        outer[:, k, 0, :, :, 0, k] = cos
        outer[:, k, 0, :, :, 1, k] = sin
        outer[:, k, 1, :, :, 1, k] = cos
        outer[:, k, 1, :, :, 0, k] = -sin
    outer = rounded(outer.reshape(2, LANES, LANES))
    x = np.arange(CELLS)
    angle = 2 * np.pi * (q[:, None] * x[None, :]) / N
    twist = np.stack([np.tile(np.cos(angle), (1, 2)), np.tile(np.sin(angle), (1, 2))]).astype(np.float32)
    angle = 2 * np.pi * ((x[:, None] * x[None, :]) % CELLS) / CELLS
    cos, sin = (t.reshape(CELLS // 4, 4, CELLS).transpose(1, 0, 2) for t in (np.cos(angle), np.sin(angle)))
    inner = np.zeros((2, 4, 2, CELLS // 4, 2, 2, CELLS))
    for k in range(2):
        inner[0, :, k, :, 0, k] = cos
        inner[0, :, k, :, 1, k] = sin
        inner[1, :, k, :, 1, k] = cos
        inner[1, :, k, :, 0, k] = -sin
    inner = rounded(inner.reshape(LANES, LANES))
    return half, outer, twist, inner


SPLIT = 4


def fold(parts):
    even = [parts[k] + parts[k + 8] for k in range(8)]
    odd = [parts[k] - parts[k + 8] for k in range(8)]
    both = [even[k] + even[k + 4] for k in range(4)]
    less = [even[k] - even[k + 4] for k in range(4)]
    yield both[0] + both[2], both[1] + both[3]
    yield both[0] - both[2], both[1] - both[3]
    half = math.sqrt(0.5)
    pairs = [((less[0], -less[2]), (less[1], -less[3]), math.pi / 4)]
    near = [(odd[k], -odd[k + 4]) for k in range(2)]
    far = [(half * (odd[k + 2] - odd[k + 6]), -half * (odd[k + 2] + odd[k + 6])) for k in range(2)]
    pairs.append(tuple((near[k][0] + far[k][0], near[k][1] + far[k][1]) for k in range(2)) + (math.pi / 8,))
    pairs.append(tuple((near[k][0] - far[k][0], near[k][1] - far[k][1]) for k in range(2)) + (5 * math.pi / 8,))
    for (real, imag), (next_real, next_imag), angle in pairs:
        cos, sin = math.cos(angle), math.sin(angle)
        turn_real, turn_imag = cos * next_real + sin * next_imag, cos * next_imag - sin * next_real
        yield real + turn_real, imag + turn_imag
        yield real - turn_real, imag - turn_imag


def half_kernel(a_hbm, b_hbm, table_hbm, out_hbm, block_ref, table_ref, fold_ref, out_ref, block_sem, table_sem, out_sem):
    rows = LANES // SPLIT
    blocks = [
        [
            pltpu.make_async_copy(
                hbm.at[pl.ds(rows * k, rows)], block_ref.at[place, pl.ds(rows * k, rows)], block_sem.at[place, k]
            )
            for k in range(SPLIT)
        ]
        for place, hbm in enumerate((a_hbm, b_hbm))
    ]
    tables = [
        pltpu.make_async_copy(
            table_hbm.at[pl.ds(N // 2 * k, N // 2)], table_ref.at[pl.ds(N // 2 * k, N // 2)], table_sem.at[k]
        )
        for k in range(2)
    ]
    for copy in blocks[0] + tables[:1] + blocks[1] + tables[1:]:
        copy.start()

    for place in range(2):
        for k in range(SPLIT):
            blocks[place][k].wait()

            def fold_rows(step, carry):
                row = pl.multiple_of(rows * k + 16 * step, 16)
                parts = [block_ref[place, pl.ds(row, 16), pl.ds(128 * p, 128)].astype(jnp.float32) for p in range(16)]
                own = pl.ds(pl.multiple_of(LANES * place + row, 16), 16)
                for kind, (first, second) in enumerate(fold(parts)):
                    fold_ref[kind, own, :128] = first.astype(jnp.bfloat16)
                    fold_ref[kind, own, 128:] = second.astype(jnp.bfloat16)
                return carry

            lax.fori_loop(0, rows // 16, fold_rows, 0, unroll=True)
    sends = []
    for kind in range(KINDS):
        if kind % 4 == 0:
            tables[kind // 4].wait()
        value = lax.dot_general(
            table_ref[pl.ds(LANES * kind, LANES), :], fold_ref[kind], NT, preferred_element_type=jnp.float32
        )
        out_ref[kind] = value.astype(jnp.bfloat16).reshape(SLABS // 2, 16, 2 * LANES)
        send = pltpu.make_async_copy(
            out_ref.at[kind], out_hbm.at[pl.ds(SLABS // 2 * (kind // 4), SLABS // 2), kind % 4], out_sem.at[kind]
        )
        send.start()
        sends.append(send)
    for send in sends:
        send.wait()


def half_transform(first, second, table):
    return pl.pallas_call(
        half_kernel,
        in_specs=[pl.BlockSpec(memory_space=pl.ANY)] * 3,
        out_specs=pl.BlockSpec(memory_space=pl.ANY),
        out_shape=jax.ShapeDtypeStruct((SLABS, GROUPS, 16, 2 * LANES), jnp.bfloat16),
        scratch_shapes=[
            pltpu.VMEM((2, LANES, N), jnp.bfloat16),
            pltpu.VMEM((N, N // 8), jnp.bfloat16),
            pltpu.VMEM((KINDS, 2 * LANES, N // 8), jnp.bfloat16),
            pltpu.VMEM((KINDS, SLABS // 2, 16, 2 * LANES), jnp.bfloat16),
            pltpu.SemaphoreType.DMA((2, SPLIT)),
            pltpu.SemaphoreType.DMA((2,)),
            pltpu.SemaphoreType.DMA((KINDS,)),
        ],
        compiler_params=pltpu.CompilerParams(vmem_limit_bytes=60 * 2**20),
        cost_estimate=pl.CostEstimate(flops=N * 512 * 512, bytes_accessed=5 * 2**20, transcendentals=0),
    )(first, second, table)


def turned(value, amount):
    amount = (SLABS * amount) % 128
    return pltpu.roll(value, amount, 1) if amount else value


def weight_kernel(spectrum_ref, nyquist_ref, weight_ref, shift_ref):
    slab, group = lax.axis_index("grid"), lax.axis_index("row")
    own = jnp.concatenate([spectrum_ref[...], jnp.broadcast_to(nyquist_ref[...], (8, N))], axis=0)
    own = jnp.concatenate([own[:, 128 * c : 128 * (c + 1)] for c in range(16)], axis=0)
    mine = 4 * (slab // (SLABS // 2)) + group
    height = CELLS + 8
    shape = ((WAVES + 1) * 16, 16 * height)
    below, along = lax.broadcasted_iota(jnp.int32, (shape[0], 1), 0), lax.broadcasted_iota(jnp.int32, shape, 1)
    wave, coarse = below // 16, below % 16
    wanted = jnp.zeros_like(wave)
    for kind in range(KINDS):
        wanted = jnp.where(mine == kind, offsets(kind, wave), wanted)
    wanted = coarse * height + jnp.where(wave < WAVES, wanted, CELLS)
    pick = jnp.where(along == wanted, 1.0, 0.0).astype(jnp.bfloat16)
    below, along = (lax.broadcasted_iota(jnp.int32, (128, 128), axis) for axis in range(2))
    moved = along // SLABS * SLABS + 2 * (along % 16) + along % SLABS // 16
    order = jnp.where(below == moved, 1.0, 0.0).astype(jnp.bfloat16)
    spread = jnp.zeros((shape[0], 128), jnp.float32)
    for _ in range(3):
        piece = own.astype(jnp.bfloat16)
        own = own - piece.astype(jnp.float32)
        picked = jnp.dot(pick, piece, preferred_element_type=jnp.float32).astype(jnp.bfloat16)
        spread += jnp.dot(picked, order, preferred_element_type=jnp.float32)
    alone = jnp.where((slab == 0) & (group == 0), 1.0, 0.0)
    shift_ref[...] = (spread[16 * WAVES :] - spread[:16]) * (alone / N**2)
    columns = [
        spread[16 * wave : 16 * (wave + 1)] * ((2.0 - alone) / N**2 if wave == 0 else 2.0 / N**2)
        for wave in range(WAVES)
    ]
    quarter = lax.broadcasted_iota(jnp.int32, (16, 128), 1) // SLABS
    for fine in range(4):
        for half in range(2):
            weight = jnp.zeros((16, 128), jnp.float32)
            for place in range(4):
                weight = jnp.where(quarter == place, turned(columns[4 * half + place], place - fine), weight)
            weight_ref[fine, :, 128 * half : 128 * (half + 1)] = weight


def spectrum_weights(spectrum, nyquist):
    return pl.pallas_call(
        weight_kernel,
        in_specs=[pl.BlockSpec(memory_space=pltpu.VMEM)] * 2,
        out_specs=[pl.BlockSpec(memory_space=pltpu.VMEM)] * 2,
        out_shape=[
            jax.ShapeDtypeStruct((4, 16, LANES), jnp.float32),
            jax.ShapeDtypeStruct((16, 128), jnp.float32),
        ],
        compiler_params=pltpu.CompilerParams(vmem_limit_bytes=16 * 2**20),
        cost_estimate=pl.CostEstimate(flops=10**9, bytes_accessed=2**20, transcendentals=0),
    )(spectrum, nyquist)


def cross_kernel(x_ref, outer_ref, twist_ref, inner_ref, weight_ref, shift_ref, out_ref, za_ref, zb_ref, ze_ref, a_ref, b_ref):
    wide = jnp.float32
    cosines, sines = (jnp.concatenate([twist_ref[k], twist_ref[k]], axis=1) for k in range(2))

    step = SLABS // 2
    nine = lax.broadcasted_iota(jnp.int32, (SLABS, LANES), 1) % 16 == WAVES
    outers = [
        jnp.concatenate([outer_ref[odd], jnp.where(nine, outer_ref[odd, :SLABS], 0.0).astype(jnp.bfloat16)], axis=0)
        for odd in range(2)
    ]

    def twist(mixed, first, odd, ref, rows):
        real, imag = mixed[first : first + step], mixed[first + step : first + 2 * step]
        cos, sin = cosines[step * odd : step * (odd + 1)], sines[step * odd : step * (odd + 1)]
        new_real = (real * cos + imag * sin).astype(jnp.bfloat16)
        new_imag = (imag * cos - real * sin).astype(jnp.bfloat16)
        for pair in range(2):
            lanes = slice(128 * pair, 128 * (pair + 1))
            ref[pair, rows, :128], ref[pair, rows, 128:] = new_real[:, lanes], new_imag[:, lanes]

    for group in range(GROUPS):
        low, high = x_ref[:step, group], x_ref[step:, group]
        for odd, cells in enumerate((low + high, low - high)):
            cells = cells.reshape(LANES, 2 * LANES)
            left = jnp.dot(outers[odd], cells[:, :LANES], preferred_element_type=wide)
            right = jnp.dot(outer_ref[odd], cells[:, LANES:], preferred_element_type=wide)
            for wave in range(WAVES):
                rows = pl.ds(SLABS * wave + step * odd, step)
                twist(left, SLABS * wave, odd, za_ref.at[group], rows)
                twist(right, SLABS * wave, odd, zb_ref.at[group], rows)
            twist(left, SLABS * WAVES, odd, ze_ref, pl.ds(SLABS * group + step * odd, step))

    quarter = lax.broadcasted_iota(jnp.int32, (16, 128), 1) // SLABS
    changes = [jnp.where(quarter == 0, turned(shift_ref[...], -fine), 0.0) for fine in range(4)]
    changes = [jnp.concatenate([change] * 2, axis=0) for change in changes]
    weights = [jnp.concatenate([weight_ref[fine]] * 2, axis=0) for fine in range(4)]
    inner = inner_ref[...]
    for pair in range(2):
        apart = lax.dot_general(inner, ze_ref[pair], NT, preferred_element_type=wide)
        for group in range(GROUPS):
            own = pl.ds(64 * group + 32 * pair, 32)
            value = lax.dot_general(inner, za_ref[group, pair], NT, preferred_element_type=wide)
            moved = turned(apart, -group)
            for part in range(2):
                for fine in range(4):
                    rows = slice(128 * part + 32 * fine, 128 * part + 32 * (fine + 1))
                    scaled = value[rows] * weights[fine]
                    changed = scaled[:, :128] + moved[rows] * changes[fine]
                    a_ref[part, fine, own, :128] = changed.astype(jnp.bfloat16)
                    a_ref[part, fine, own, 128:] = scaled[:, 128:].astype(jnp.bfloat16)
            value = lax.dot_general(inner, zb_ref[group, pair], NT, preferred_element_type=wide)
            for part in range(2):
                for fine in range(4):
                    rows = slice(128 * part + 32 * fine, 128 * part + 32 * (fine + 1))
                    b_ref[part, fine, own] = value[rows].astype(jnp.bfloat16)

    product = jnp.zeros((LANES, LANES), wide)
    for part in range(2):
        for fine in range(4):
            product += lax.dot_general(a_ref[part, fine], b_ref[part, fine], NT, preferred_element_type=wide)
    below = lax.broadcasted_iota(jnp.int32, (LANES, LANES), 0)
    along = lax.broadcasted_iota(jnp.int32, (LANES, LANES), 1)
    product = jnp.where(below % 16 == along % 16, product, 0.0)
    rows = jnp.concatenate([product[16 * k : 16 * (k + 1)].sum(0, keepdims=True) for k in range(16)], axis=0)
    below, along = (lax.broadcasted_iota(jnp.int32, (LANES, 128), axis) for axis in range(2))
    gather = jnp.where(below // 16 == along % 16, 1.0, 0.0).astype(jnp.bfloat16)
    total = jnp.zeros((16, 128), wide)
    for _ in range(3):
        piece = rows.astype(jnp.bfloat16)
        rows = rows - piece.astype(wide)
        total += jnp.dot(piece, gather, preferred_element_type=wide)
    below, along = (lax.broadcasted_iota(jnp.int32, (16, 128), axis) for axis in range(2))
    total = jnp.where(below % ROWS == along // 16, total, 0.0)
    sums = [total[ROWS * group : ROWS * (group + 1)].sum(0, keepdims=True) for group in range(GROUPS)]
    for slab in range(SLABS):
        for group in range(GROUPS):
            out_ref[slab * GROUPS + group] = sums[group]


def cross_partial(arrived, outer, twist, inner, weight, shift):
    return pl.pallas_call(
        cross_kernel,
        in_specs=[pl.BlockSpec(memory_space=pltpu.VMEM)] * 6,
        out_specs=pl.BlockSpec(memory_space=pltpu.VMEM),
        out_shape=jax.ShapeDtypeStruct((SLABS * GROUPS, 1, 128), jnp.float32),
        scratch_shapes=[
            pltpu.VMEM((GROUPS, 2, LANES, LANES), jnp.bfloat16),
            pltpu.VMEM((GROUPS, 2, LANES, LANES), jnp.bfloat16),
            pltpu.VMEM((2, 128, LANES), jnp.bfloat16),
            pltpu.VMEM((2, 4, LANES, LANES), jnp.bfloat16),
            pltpu.VMEM((2, 4, LANES, LANES), jnp.bfloat16),
        ],
        compiler_params=pltpu.CompilerParams(vmem_limit_bytes=36 * 2**20),
        cost_estimate=pl.CostEstimate(flops=3 * 10**9, bytes_accessed=5 * 2**20, transcendentals=0),
    )(arrived, outer, twist, inner, weight, shift)


def lookup(indices, table):
    onehot = indices[:, None] == jnp.arange(table.shape[0], dtype=jnp.int32)[None, :]
    return jnp.sum(jnp.where(onehot, table[None, :], 0.0), axis=1)


def shards(first_block, second_block, spectrum, first_ids, second_ids, error_scale):
    half, outer, twist, inner = (jnp.asarray(t) for t in make_tables())
    sent = half_transform(first_block.reshape(LANES, N), second_block.reshape(LANES, N), half)
    sent = sent.reshape(SLABS * GROUPS, 16, 2 * LANES)
    arrived = lax.all_to_all(sent, EVERY, 0, 0, tiled=True)
    nyquist = lax.ppermute(spectrum[:1], "grid", [(SLABS // 2, 0)])
    weight, shift = spectrum_weights(spectrum, nyquist)
    arrived = arrived.reshape(SLABS, GROUPS, 16, 2 * LANES)
    partial = cross_partial(arrived, outer, twist, inner, weight, shift)
    partial = lax.all_to_all(partial, EVERY, 0, 0, tiled=True)
    cross = partial.sum((0, 1))[:64].reshape(ROWS, GROUPS * ROWS)
    scale_first = lookup(first_ids, error_scale)
    scale_second = lookup(second_ids, error_scale)
    return cross / (N * scale_first[:, None] * scale_second[None, :])


def solution(mesh):
    return jax.shard_map(
        shards,
        mesh=mesh,
        in_specs=(
            P("row", "grid", None),
            P("row", "grid", None),
            P("grid", None),
            P("row"),
            P(),
            P(),
        ),
        out_specs=P("row", None),
        check_vma=False,
    )
```

```python
import functools
import math

import jax
import jax.numpy as jnp
import ml_dtypes
import numpy as np
from jax import lax
from jax.experimental import pallas as pl
from jax.experimental.pallas import tpu as pltpu
from jax.sharding import PartitionSpec as P

N = 2048
SLABS = 32
GROUPS = 4
CELLS = N // SLABS
ROWS = 4
WAVES = 8
KINDS = 8
LANES = ROWS * CELLS
EVERY = ("row", "grid")

NT = (((1,), (1,)), ((), ()))


def rounded(array):
    return np.asarray(array, np.float64).astype(ml_dtypes.bfloat16)


BASES = (0, 4, 2, 10, 1, 9, 5, 13)


def offsets(kind, j):
    if kind < 2:
        return 8 * j + BASES[kind]
    return 16 * (j // 2) + BASES[kind] + (16 - 2 * BASES[kind]) * (j % 2)


@functools.lru_cache(None)
def make_tables():
    y = np.arange(N // 8)
    j = np.arange(WAVES)
    half = np.zeros((KINDS, SLABS // 2, 2, WAVES, N // 8))
    for kind in range(KINDS):
        for slab in range(SLABS // 2):
            waves = CELLS * (slab + SLABS // 2 * (kind // 4)) + offsets(kind, j)
            if kind < 2:
                angle = 2 * np.pi * ((waves[:, None] * y[None, :]) % N) / N
                half[kind, slab, 0] = np.cos(angle)
                half[kind, slab, 1] = -np.sin(angle)
                continue
            mirror = waves % 16 != BASES[kind]
            waves = np.where(mirror, N - waves, waves)
            angle = 2 * np.pi * ((waves[:, None] * y[None, : N // 16]) % N) / N
            sign = np.where(mirror, -1, 1)[:, None]
            half[kind, slab, 0] = np.concatenate([np.cos(angle), np.sin(angle)], 1)
            half[kind, slab, 1] = sign * np.concatenate([-np.sin(angle), np.cos(angle)], 1)
    half[0, 0, 1, 0] = (-1.0) ** y
    half = rounded(half.reshape(N, N // 8))
    q = np.arange(SLABS).reshape(SLABS // 2, 2).T.reshape(SLABS)
    angle = 2 * np.pi * ((q[:, None] * np.arange(SLABS // 2)[None, :]) % SLABS) / SLABS
    cos, sin = np.cos(angle).reshape(2, SLABS // 2, -1), np.sin(angle).reshape(2, SLABS // 2, -1)
    outer = np.zeros((2, WAVES, 2, SLABS // 2, SLABS // 2, 2, WAVES))
    for k in range(WAVES):
        outer[:, k, 0, :, :, 0, k] = cos
        outer[:, k, 0, :, :, 1, k] = sin
        outer[:, k, 1, :, :, 1, k] = cos
        outer[:, k, 1, :, :, 0, k] = -sin
    outer = rounded(outer.reshape(2, LANES, LANES))
    x = np.arange(CELLS)
    angle = 2 * np.pi * (q[:, None] * x[None, :]) / N
    twist = np.stack([np.tile(np.cos(angle), (1, 2)), np.tile(np.sin(angle), (1, 2))]).astype(np.float32)
    angle = 2 * np.pi * ((x[:, None] * x[None, :]) % CELLS) / CELLS
    cos, sin = (t.reshape(CELLS // 4, 4, CELLS).transpose(1, 0, 2) for t in (np.cos(angle), np.sin(angle)))
    inner = np.zeros((2, 4, 2, CELLS // 4, 2, 2, CELLS))
    for k in range(2):
        inner[0, :, k, :, 0, k] = cos
        inner[0, :, k, :, 1, k] = sin
        inner[1, :, k, :, 1, k] = cos
        inner[1, :, k, :, 0, k] = -sin
    inner = rounded(inner.reshape(LANES, LANES))
    return half, outer, twist, inner


SPLIT = 4


def fold(parts):
    even = [parts[k] + parts[k + 8] for k in range(8)]
    odd = [parts[k] - parts[k + 8] for k in range(8)]
    both = [even[k] + even[k + 4] for k in range(4)]
    less = [even[k] - even[k + 4] for k in range(4)]
    yield both[0] + both[2], both[1] + both[3]
    yield both[0] - both[2], both[1] - both[3]
    half = math.sqrt(0.5)
    pairs = [((less[0], -less[2]), (less[1], -less[3]), math.pi / 4)]
    near = [(odd[k], -odd[k + 4]) for k in range(2)]
    far = [(half * (odd[k + 2] - odd[k + 6]), -half * (odd[k + 2] + odd[k + 6])) for k in range(2)]
    pairs.append(tuple((near[k][0] + far[k][0], near[k][1] + far[k][1]) for k in range(2)) + (math.pi / 8,))
    pairs.append(tuple((near[k][0] - far[k][0], near[k][1] - far[k][1]) for k in range(2)) + (5 * math.pi / 8,))
    for (real, imag), (next_real, next_imag), angle in pairs:
        cos, sin = math.cos(angle), math.sin(angle)
        turn_real, turn_imag = cos * next_real + sin * next_imag, cos * next_imag - sin * next_real
        yield real + turn_real, imag + turn_imag
        yield real - turn_real, imag - turn_imag


def half_kernel(a_hbm, b_hbm, table_hbm, out_hbm, block_ref, table_ref, fold_ref, out_ref, block_sem, table_sem, out_sem):
    rows = LANES // SPLIT
    blocks = [
        [
            pltpu.make_async_copy(
                hbm.at[pl.ds(rows * k, rows)], block_ref.at[place, pl.ds(rows * k, rows)], block_sem.at[place, k]
            )
            for k in range(SPLIT)
        ]
        for place, hbm in enumerate((a_hbm, b_hbm))
    ]
    tables = [
        pltpu.make_async_copy(
            table_hbm.at[pl.ds(N // 2 * k, N // 2)], table_ref.at[pl.ds(N // 2 * k, N // 2)], table_sem.at[k]
        )
        for k in range(2)
    ]
    for copy in blocks[0] + blocks[1] + tables:
        copy.start()

    for place in range(2):
        for k in range(SPLIT):
            blocks[place][k].wait()

            def fold_rows(step, carry):
                row = pl.multiple_of(rows * k + 16 * step, 16)
                parts = [block_ref[place, pl.ds(row, 16), pl.ds(128 * p, 128)].astype(jnp.float32) for p in range(16)]
                own = pl.ds(pl.multiple_of(LANES * place + row, 16), 16)
                for kind, (first, second) in enumerate(fold(parts)):
                    fold_ref[kind, own, :128] = first.astype(jnp.bfloat16)
                    fold_ref[kind, own, 128:] = second.astype(jnp.bfloat16)
                return carry

            lax.fori_loop(0, rows // 16, fold_rows, 0, unroll=True)
    sends = []
    for kind in range(KINDS):
        if kind % 4 == 0:
            tables[kind // 4].wait()
        value = lax.dot_general(
            table_ref[pl.ds(LANES * kind, LANES), :], fold_ref[kind], NT, preferred_element_type=jnp.float32
        )
        out_ref[kind] = value.astype(jnp.bfloat16).reshape(SLABS // 2, 16, 2 * LANES)
        send = pltpu.make_async_copy(
            out_ref.at[kind], out_hbm.at[kind % 4, pl.ds(SLABS // 2 * (kind // 4), SLABS // 2)], out_sem.at[kind]
        )
        send.start()
        sends.append(send)
    for send in sends:
        send.wait()


def half_transform(first, second, table):
    return pl.pallas_call(
        half_kernel,
        in_specs=[pl.BlockSpec(memory_space=pl.ANY)] * 3,
        out_specs=pl.BlockSpec(memory_space=pl.ANY),
        out_shape=jax.ShapeDtypeStruct((GROUPS, SLABS, 16, 2 * LANES), jnp.bfloat16),
        scratch_shapes=[
            pltpu.VMEM((2, LANES, N), jnp.bfloat16),
            pltpu.VMEM((N, N // 8), jnp.bfloat16),
            pltpu.VMEM((KINDS, 2 * LANES, N // 8), jnp.bfloat16),
            pltpu.VMEM((KINDS, SLABS // 2, 16, 2 * LANES), jnp.bfloat16),
            pltpu.SemaphoreType.DMA((2, SPLIT)),
            pltpu.SemaphoreType.DMA((2,)),
            pltpu.SemaphoreType.DMA((KINDS,)),
        ],
        compiler_params=pltpu.CompilerParams(vmem_limit_bytes=60 * 2**20),
        cost_estimate=pl.CostEstimate(flops=N * 512 * 512, bytes_accessed=5 * 2**20, transcendentals=0),
    )(first, second, table)


def turned(value, amount):
    amount = (SLABS * amount) % 128
    return pltpu.roll(value, amount, 1) if amount else value


def weight_kernel(spectrum_ref, nyquist_ref, weight_ref, shift_ref):
    slab, group = lax.axis_index("grid"), lax.axis_index("row")
    own = jnp.concatenate([spectrum_ref[...], jnp.broadcast_to(nyquist_ref[...], (8, N))], axis=0)
    own = jnp.concatenate([own[:, 128 * c : 128 * (c + 1)] for c in range(16)], axis=0)
    mine = 4 * (slab // (SLABS // 2)) + group
    height = CELLS + 8
    shape = ((WAVES + 1) * 16, 16 * height)
    below, along = lax.broadcasted_iota(jnp.int32, (shape[0], 1), 0), lax.broadcasted_iota(jnp.int32, shape, 1)
    wave, coarse = below // 16, below % 16
    wanted = jnp.zeros_like(wave)
    for kind in range(KINDS):
        wanted = jnp.where(mine == kind, offsets(kind, wave), wanted)
    wanted = coarse * height + jnp.where(wave < WAVES, wanted, CELLS)
    pick = jnp.where(along == wanted, 1.0, 0.0).astype(jnp.bfloat16)
    below, along = (lax.broadcasted_iota(jnp.int32, (128, 128), axis) for axis in range(2))
    moved = along // SLABS * SLABS + 2 * (along % 16) + along % SLABS // 16
    order = jnp.where(below == moved, 1.0, 0.0).astype(jnp.bfloat16)
    spread = jnp.zeros((shape[0], 128), jnp.float32)
    for _ in range(3):
        piece = own.astype(jnp.bfloat16)
        own = own - piece.astype(jnp.float32)
        picked = jnp.dot(pick, piece, preferred_element_type=jnp.float32).astype(jnp.bfloat16)
        spread += jnp.dot(picked, order, preferred_element_type=jnp.float32)
    alone = jnp.where((slab == 0) & (group == 0), 1.0, 0.0)
    shift_ref[...] = (spread[16 * WAVES :] - spread[:16]) * (alone / N**2)
    columns = [
        spread[16 * wave : 16 * (wave + 1)] * ((2.0 - alone) / N**2 if wave == 0 else 2.0 / N**2)
        for wave in range(WAVES)
    ]
    quarter = lax.broadcasted_iota(jnp.int32, (16, 128), 1) // SLABS
    for fine in range(4):
        for half in range(2):
            weight = jnp.zeros((16, 128), jnp.float32)
            for place in range(4):
                weight = jnp.where(quarter == place, turned(columns[4 * half + place], place - fine), weight)
            weight_ref[fine, :, 128 * half : 128 * (half + 1)] = weight


def spectrum_weights(spectrum, nyquist):
    return pl.pallas_call(
        weight_kernel,
        in_specs=[pl.BlockSpec(memory_space=pltpu.VMEM)] * 2,
        out_specs=[pl.BlockSpec(memory_space=pltpu.VMEM)] * 2,
        out_shape=[
            jax.ShapeDtypeStruct((4, 16, LANES), jnp.float32),
            jax.ShapeDtypeStruct((16, 128), jnp.float32),
        ],
        compiler_params=pltpu.CompilerParams(vmem_limit_bytes=16 * 2**20),
        cost_estimate=pl.CostEstimate(flops=10**9, bytes_accessed=2**20, transcendentals=0),
    )(spectrum, nyquist)


def cross_kernel(x_ref, outer_ref, twist_ref, inner_ref, weight_ref, shift_ref, out_ref, za_ref, zb_ref, ze_ref, a_ref, b_ref):
    wide = jnp.float32
    cosines, sines = (jnp.concatenate([twist_ref[k], twist_ref[k]], axis=1) for k in range(2))

    step = SLABS // 2
    nine = lax.broadcasted_iota(jnp.int32, (SLABS, LANES), 1) % 16 == WAVES
    outers = [
        jnp.concatenate([outer_ref[odd], jnp.where(nine, outer_ref[odd, :SLABS], 0.0).astype(jnp.bfloat16)], axis=0)
        for odd in range(2)
    ]

    def twist(mixed, first, odd, ref, rows):
        real, imag = mixed[first : first + step], mixed[first + step : first + 2 * step]
        cos, sin = cosines[step * odd : step * (odd + 1)], sines[step * odd : step * (odd + 1)]
        new_real = (real * cos + imag * sin).astype(jnp.bfloat16)
        new_imag = (imag * cos - real * sin).astype(jnp.bfloat16)
        for pair in range(2):
            lanes = slice(128 * pair, 128 * (pair + 1))
            ref[pair, rows, :128], ref[pair, rows, 128:] = new_real[:, lanes], new_imag[:, lanes]

    inner = inner_ref[...]

    def right_cells(group):
        for pair in range(2):
            own = pl.ds(64 * group + 32 * pair, 32)
            value = lax.dot_general(inner, zb_ref[group, pair], NT, preferred_element_type=wide)
            for part in range(2):
                for fine in range(4):
                    rows = slice(128 * part + 32 * fine, 128 * part + 32 * (fine + 1))
                    b_ref[part, fine, own] = value[rows].astype(jnp.bfloat16)

    for group in range(GROUPS):
        low, high = x_ref[group, :step], x_ref[group, step:]
        for odd, cells in enumerate((low + high, low - high)):
            cells = cells.reshape(LANES, 2 * LANES)
            left = jnp.dot(outers[odd], cells[:, :LANES], preferred_element_type=wide)
            right = jnp.dot(outer_ref[odd], cells[:, LANES:], preferred_element_type=wide)
            for wave in range(WAVES):
                rows = pl.ds(SLABS * wave + step * odd, step)
                twist(left, SLABS * wave, odd, za_ref.at[group], rows)
                twist(right, SLABS * wave, odd, zb_ref.at[group], rows)
            twist(left, SLABS * WAVES, odd, ze_ref, pl.ds(SLABS * group + step * odd, step))
        if group:
            right_cells(group - 1)
    right_cells(GROUPS - 1)

    quarter = lax.broadcasted_iota(jnp.int32, (16, 128), 1) // SLABS
    changes = [jnp.where(quarter == 0, turned(shift_ref[...], -fine), 0.0) for fine in range(4)]
    changes = [jnp.concatenate([change] * 2, axis=0) for change in changes]
    weights = [jnp.concatenate([weight_ref[fine]] * 2, axis=0) for fine in range(4)]
    for pair in range(2):
        apart = lax.dot_general(inner, ze_ref[pair], NT, preferred_element_type=wide)
        for group in range(GROUPS):
            own = pl.ds(64 * group + 32 * pair, 32)
            value = lax.dot_general(inner, za_ref[group, pair], NT, preferred_element_type=wide)
            moved = turned(apart, -group)
            for part in range(2):
                for fine in range(4):
                    rows = slice(128 * part + 32 * fine, 128 * part + 32 * (fine + 1))
                    scaled = value[rows] * weights[fine]
                    changed = scaled[:, :128] + moved[rows] * changes[fine]
                    a_ref[part, fine, own, :128] = changed.astype(jnp.bfloat16)
                    a_ref[part, fine, own, 128:] = scaled[:, 128:].astype(jnp.bfloat16)

    product = jnp.zeros((LANES, LANES), wide)
    for part in range(2):
        for fine in range(4):
            product += lax.dot_general(a_ref[part, fine], b_ref[part, fine], NT, preferred_element_type=wide)
    below = lax.broadcasted_iota(jnp.int32, (LANES, LANES), 0)
    along = lax.broadcasted_iota(jnp.int32, (LANES, LANES), 1)
    product = jnp.where(below % 16 == along % 16, product, 0.0)
    rows = jnp.concatenate([product[16 * k : 16 * (k + 1)].sum(0, keepdims=True) for k in range(16)], axis=0)
    below, along = (lax.broadcasted_iota(jnp.int32, (LANES, 128), axis) for axis in range(2))
    gather = jnp.where(below // 16 == along % 16, 1.0, 0.0).astype(jnp.bfloat16)
    total = jnp.zeros((16, 128), wide)
    for _ in range(3):
        piece = rows.astype(jnp.bfloat16)
        rows = rows - piece.astype(wide)
        total += jnp.dot(piece, gather, preferred_element_type=wide)
    below, along = (lax.broadcasted_iota(jnp.int32, (16, 128), axis) for axis in range(2))
    total = jnp.where(below % ROWS == along // 16, total, 0.0)
    sums = [total[ROWS * group : ROWS * (group + 1)].sum(0, keepdims=True) for group in range(GROUPS)]
    for slab in range(SLABS):
        for group in range(GROUPS):
            out_ref[group * SLABS + slab] = sums[group]


def cross_partial(arrived, outer, twist, inner, weight, shift):
    return pl.pallas_call(
        cross_kernel,
        in_specs=[pl.BlockSpec(memory_space=pltpu.VMEM)] * 6,
        out_specs=pl.BlockSpec(memory_space=pltpu.VMEM),
        out_shape=jax.ShapeDtypeStruct((SLABS * GROUPS, 1, 128), jnp.float32),
        scratch_shapes=[
            pltpu.VMEM((GROUPS, 2, LANES, LANES), jnp.bfloat16),
            pltpu.VMEM((GROUPS, 2, LANES, LANES), jnp.bfloat16),
            pltpu.VMEM((2, 128, LANES), jnp.bfloat16),
            pltpu.VMEM((2, 4, LANES, LANES), jnp.bfloat16),
            pltpu.VMEM((2, 4, LANES, LANES), jnp.bfloat16),
        ],
        compiler_params=pltpu.CompilerParams(vmem_limit_bytes=36 * 2**20),
        cost_estimate=pl.CostEstimate(flops=3 * 10**9, bytes_accessed=5 * 2**20, transcendentals=0),
    )(arrived, outer, twist, inner, weight, shift)


def lookup(indices, table):
    onehot = indices[:, None] == jnp.arange(table.shape[0], dtype=jnp.int32)[None, :]
    return jnp.sum(jnp.where(onehot, table[None, :], 0.0), axis=1)


def shards(first_block, second_block, spectrum, first_ids, second_ids, error_scale):
    half, outer, twist, inner = (jnp.asarray(t) for t in make_tables())
    sent = half_transform(first_block.reshape(LANES, N), second_block.reshape(LANES, N), half)
    sent = sent.reshape(SLABS * GROUPS, 16, 2 * LANES)
    arrived = lax.all_to_all(sent, EVERY, 0, 0, tiled=True)
    nyquist = lax.ppermute(spectrum[:1], "grid", [(SLABS // 2, 0)])
    weight, shift = spectrum_weights(spectrum, nyquist)
    arrived = arrived.reshape(GROUPS, SLABS, 16, 2 * LANES)
    partial = cross_partial(arrived, outer, twist, inner, weight, shift)
    factor = 1.0 / (N * lookup(first_ids, error_scale)[:, None] * lookup(second_ids, error_scale)[None, :])
    partial, factor = lax.optimization_barrier((partial, factor))
    partial = lax.all_to_all(partial, EVERY, 0, 0, tiled=True)
    return partial.sum((0, 1))[:64].reshape(ROWS, GROUPS * ROWS) * factor


def solution(mesh):
    return jax.shard_map(
        shards,
        mesh=mesh,
        in_specs=(
            P("row", "grid", None),
            P("row", "grid", None),
            P("grid", None),
            P("row"),
            P(),
            P(),
        ),
        out_specs=P("row", None),
        check_vma=False,
    )
```

```python
import functools
import math

import jax
import jax.numpy as jnp
import ml_dtypes
import numpy as np
from jax import lax
from jax.experimental import pallas as pl
from jax.experimental.pallas import tpu as pltpu
from jax.sharding import PartitionSpec as P

N = 2048
SLABS = 32
GROUPS = 4
CELLS = N // SLABS
ROWS = 4
WAVES = 8
KINDS = 8
LANES = ROWS * CELLS
EVERY = ("row", "grid")

NT = (((1,), (1,)), ((), ()))


def rounded(array):
    return np.asarray(array, np.float64).astype(ml_dtypes.bfloat16)


BASES = (0, 4, 2, 10, 1, 9, 5, 13)


def offsets(kind, j):
    if kind < 2:
        return 8 * j + BASES[kind]
    return 16 * (j // 2) + BASES[kind] + (16 - 2 * BASES[kind]) * (j % 2)


@functools.lru_cache(None)
def make_tables():
    y = np.arange(N // 8)
    j = np.arange(WAVES)
    half = np.zeros((KINDS, SLABS // 2, 2, WAVES, N // 8))
    for kind in range(KINDS):
        for slab in range(SLABS // 2):
            waves = CELLS * (slab + SLABS // 2 * (kind // 4)) + offsets(kind, j)
            if kind < 2:
                angle = 2 * np.pi * ((waves[:, None] * y[None, :]) % N) / N
                half[kind, slab, 0] = np.cos(angle)
                half[kind, slab, 1] = -np.sin(angle)
                continue
            mirror = waves % 16 != BASES[kind]
            waves = np.where(mirror, N - waves, waves)
            angle = 2 * np.pi * ((waves[:, None] * y[None, : N // 16]) % N) / N
            sign = np.where(mirror, -1, 1)[:, None]
            half[kind, slab, 0] = np.concatenate([np.cos(angle), np.sin(angle)], 1)
            half[kind, slab, 1] = sign * np.concatenate([-np.sin(angle), np.cos(angle)], 1)
    half[0, 0, 1, 0] = (-1.0) ** y
    half = rounded(half.reshape(N, N // 8))
    q = np.arange(SLABS).reshape(SLABS // 2, 2).T.reshape(SLABS)
    angle = 2 * np.pi * ((q[:, None] * np.arange(SLABS // 2)[None, :]) % SLABS) / SLABS
    cos, sin = np.cos(angle).reshape(2, SLABS // 2, -1), np.sin(angle).reshape(2, SLABS // 2, -1)
    outer = np.zeros((2, WAVES, 2, SLABS // 2, SLABS // 2, 2, WAVES))
    for k in range(WAVES):
        outer[:, k, 0, :, :, 0, k] = cos
        outer[:, k, 0, :, :, 1, k] = sin
        outer[:, k, 1, :, :, 1, k] = cos
        outer[:, k, 1, :, :, 0, k] = -sin
    outer = rounded(outer.reshape(2, LANES, LANES))
    x = np.arange(CELLS)
    angle = 2 * np.pi * (q[:, None] * x[None, :]) / N
    twist = np.stack([np.tile(np.cos(angle), (1, 2)), np.tile(np.sin(angle), (1, 2))]).astype(np.float32)
    angle = 2 * np.pi * ((x[:, None] * x[None, :]) % CELLS) / CELLS
    cos, sin = (t.reshape(CELLS // 4, 4, CELLS).transpose(1, 0, 2) for t in (np.cos(angle), np.sin(angle)))
    inner = np.zeros((2, 4, 2, CELLS // 4, 2, 2, CELLS))
    for k in range(2):
        inner[0, :, k, :, 0, k] = cos
        inner[0, :, k, :, 1, k] = sin
        inner[1, :, k, :, 1, k] = cos
        inner[1, :, k, :, 0, k] = -sin
    inner = rounded(inner.reshape(LANES, LANES))
    return half, outer, twist, inner


SPLIT = 4


def fold(parts):
    even = [parts[k] + parts[k + 8] for k in range(8)]
    odd = [parts[k] - parts[k + 8] for k in range(8)]
    both = [even[k] + even[k + 4] for k in range(4)]
    less = [even[k] - even[k + 4] for k in range(4)]
    yield both[0] + both[2], both[1] + both[3]
    yield both[0] - both[2], both[1] - both[3]
    half = math.sqrt(0.5)
    pairs = [((less[0], -less[2]), (less[1], -less[3]), math.pi / 4)]
    near = [(odd[k], -odd[k + 4]) for k in range(2)]
    far = [(half * (odd[k + 2] - odd[k + 6]), -half * (odd[k + 2] + odd[k + 6])) for k in range(2)]
    pairs.append(tuple((near[k][0] + far[k][0], near[k][1] + far[k][1]) for k in range(2)) + (math.pi / 8,))
    pairs.append(tuple((near[k][0] - far[k][0], near[k][1] - far[k][1]) for k in range(2)) + (5 * math.pi / 8,))
    for (real, imag), (next_real, next_imag), angle in pairs:
        cos, sin = math.cos(angle), math.sin(angle)
        turn_real, turn_imag = cos * next_real + sin * next_imag, cos * next_imag - sin * next_real
        yield real + turn_real, imag + turn_imag
        yield real - turn_real, imag - turn_imag


def half_kernel(a_hbm, b_hbm, table_hbm, out_hbm, block_ref, table_ref, fold_ref, out_ref, block_sem, table_sem, out_sem):
    rows = LANES // SPLIT
    blocks = [
        [
            pltpu.make_async_copy(
                hbm.at[pl.ds(rows * k, rows)], block_ref.at[place, pl.ds(rows * k, rows)], block_sem.at[place, k]
            )
            for k in range(SPLIT)
        ]
        for place, hbm in enumerate((a_hbm, b_hbm))
    ]
    tables = [
        pltpu.make_async_copy(
            table_hbm.at[pl.ds(LANES * k, LANES)], table_ref.at[pl.ds(LANES * k, LANES)], table_sem.at[k]
        )
        for k in range(KINDS)
    ]
    for copy in blocks[0] + blocks[1] + tables:
        copy.start()

    for place in range(2):
        for k in range(SPLIT):
            blocks[place][k].wait()

            def fold_rows(step, carry):
                row = pl.multiple_of(rows * k + 16 * step, 16)
                parts = [block_ref[place, pl.ds(row, 16), pl.ds(128 * p, 128)].astype(jnp.float32) for p in range(16)]
                own = pl.ds(pl.multiple_of(LANES * place + row, 16), 16)
                for kind, (first, second) in enumerate(fold(parts)):
                    fold_ref[kind, own, :128] = first.astype(jnp.bfloat16)
                    fold_ref[kind, own, 128:] = second.astype(jnp.bfloat16)
                return carry

            lax.fori_loop(0, rows // 16, fold_rows, 0, unroll=True)
    sends = []
    for kind in range(KINDS):
        tables[kind].wait()
        value = lax.dot_general(
            table_ref[pl.ds(LANES * kind, LANES), :], fold_ref[kind], NT, preferred_element_type=jnp.float32
        )
        out_ref[kind] = value.astype(jnp.bfloat16).reshape(SLABS // 2, 16, 2 * LANES)
        send = pltpu.make_async_copy(
            out_ref.at[kind], out_hbm.at[kind % 4, pl.ds(SLABS // 2 * (kind // 4), SLABS // 2)], out_sem.at[kind]
        )
        send.start()
        sends.append(send)
    for send in sends:
        send.wait()


def half_transform(first, second, table):
    return pl.pallas_call(
        half_kernel,
        in_specs=[pl.BlockSpec(memory_space=pl.ANY)] * 3,
        out_specs=pl.BlockSpec(memory_space=pl.ANY),
        out_shape=jax.ShapeDtypeStruct((GROUPS, SLABS, 16, 2 * LANES), jnp.bfloat16),
        scratch_shapes=[
            pltpu.VMEM((2, LANES, N), jnp.bfloat16),
            pltpu.VMEM((N, N // 8), jnp.bfloat16),
            pltpu.VMEM((KINDS, 2 * LANES, N // 8), jnp.bfloat16),
            pltpu.VMEM((KINDS, SLABS // 2, 16, 2 * LANES), jnp.bfloat16),
            pltpu.SemaphoreType.DMA((2, SPLIT)),
            pltpu.SemaphoreType.DMA((KINDS,)),
            pltpu.SemaphoreType.DMA((KINDS,)),
        ],
        compiler_params=pltpu.CompilerParams(vmem_limit_bytes=60 * 2**20),
        cost_estimate=pl.CostEstimate(flops=N * 512 * 512, bytes_accessed=5 * 2**20, transcendentals=0),
    )(first, second, table)


def turned(value, amount):
    amount = (SLABS * amount) % 128
    return pltpu.roll(value, amount, 1) if amount else value


def weight_kernel(spectrum_ref, nyquist_ref, weight_ref, shift_ref):
    slab, group = lax.axis_index("grid"), lax.axis_index("row")
    own = jnp.concatenate([spectrum_ref[...], jnp.broadcast_to(nyquist_ref[...], (8, N))], axis=0)
    own = jnp.concatenate([own[:, 128 * c : 128 * (c + 1)] for c in range(16)], axis=0)
    mine = 4 * (slab // (SLABS // 2)) + group
    height = CELLS + 8
    shape = ((WAVES + 1) * 16, 16 * height)
    below, along = lax.broadcasted_iota(jnp.int32, (shape[0], 1), 0), lax.broadcasted_iota(jnp.int32, shape, 1)
    wave, coarse = below // 16, below % 16
    wanted = jnp.zeros_like(wave)
    for kind in range(KINDS):
        wanted = jnp.where(mine == kind, offsets(kind, wave), wanted)
    wanted = coarse * height + jnp.where(wave < WAVES, wanted, CELLS)
    pick = jnp.where(along == wanted, 1.0, 0.0).astype(jnp.bfloat16)
    below, along = (lax.broadcasted_iota(jnp.int32, (128, 128), axis) for axis in range(2))
    moved = along // SLABS * SLABS + 2 * (along % 16) + along % SLABS // 16
    order = jnp.where(below == moved, 1.0, 0.0).astype(jnp.bfloat16)
    spread = jnp.zeros((shape[0], 128), jnp.float32)
    for _ in range(3):
        piece = own.astype(jnp.bfloat16)
        own = own - piece.astype(jnp.float32)
        picked = jnp.dot(pick, piece, preferred_element_type=jnp.float32).astype(jnp.bfloat16)
        spread += jnp.dot(picked, order, preferred_element_type=jnp.float32)
    alone = jnp.where((slab == 0) & (group == 0), 1.0, 0.0)
    shift_ref[...] = (spread[16 * WAVES :] - spread[:16]) * (alone / N**2)
    columns = [
        spread[16 * wave : 16 * (wave + 1)] * ((2.0 - alone) / N**2 if wave == 0 else 2.0 / N**2)
        for wave in range(WAVES)
    ]
    quarter = lax.broadcasted_iota(jnp.int32, (16, 128), 1) // SLABS
    for fine in range(4):
        for half in range(2):
            weight = jnp.zeros((16, 128), jnp.float32)
            for place in range(4):
                weight = jnp.where(quarter == place, turned(columns[4 * half + place], place - fine), weight)
            weight_ref[fine, :, 128 * half : 128 * (half + 1)] = weight


def spectrum_weights(spectrum, nyquist):
    return pl.pallas_call(
        weight_kernel,
        in_specs=[pl.BlockSpec(memory_space=pltpu.VMEM)] * 2,
        out_specs=[pl.BlockSpec(memory_space=pltpu.VMEM)] * 2,
        out_shape=[
            jax.ShapeDtypeStruct((4, 16, LANES), jnp.float32),
            jax.ShapeDtypeStruct((16, 128), jnp.float32),
        ],
        compiler_params=pltpu.CompilerParams(vmem_limit_bytes=16 * 2**20),
        cost_estimate=pl.CostEstimate(flops=10**9, bytes_accessed=2**20, transcendentals=0),
    )(spectrum, nyquist)


def cross_kernel(x_ref, outer_ref, twist_ref, inner_ref, weight_ref, shift_ref, out_ref, za_ref, zb_ref, ze_ref, a_ref, b_ref):
    wide = jnp.float32
    cosines, sines = (jnp.concatenate([twist_ref[k], twist_ref[k]], axis=1) for k in range(2))

    step = SLABS // 2
    nine = lax.broadcasted_iota(jnp.int32, (SLABS, LANES), 1) % 16 == WAVES
    outers = [
        jnp.concatenate([outer_ref[odd], jnp.where(nine, outer_ref[odd, :SLABS], 0.0).astype(jnp.bfloat16)], axis=0)
        for odd in range(2)
    ]

    def twist(mixed, first, odd, ref, rows):
        real, imag = mixed[first : first + step], mixed[first + step : first + 2 * step]
        cos, sin = cosines[step * odd : step * (odd + 1)], sines[step * odd : step * (odd + 1)]
        new_real = (real * cos + imag * sin).astype(jnp.bfloat16)
        new_imag = (imag * cos - real * sin).astype(jnp.bfloat16)
        for pair in range(2):
            lanes = slice(128 * pair, 128 * (pair + 1))
            ref[pair, rows, :128], ref[pair, rows, 128:] = new_real[:, lanes], new_imag[:, lanes]

    inner = inner_ref[...]

    def right_cells(group):
        for pair in range(2):
            own = pl.ds(64 * group + 32 * pair, 32)
            value = lax.dot_general(inner, zb_ref[group, pair], NT, preferred_element_type=wide)
            for part in range(2):
                for fine in range(4):
                    rows = slice(128 * part + 32 * fine, 128 * part + 32 * (fine + 1))
                    b_ref[part, fine, own] = value[rows].astype(jnp.bfloat16)

    for group in range(GROUPS):
        low, high = x_ref[group, :step], x_ref[group, step:]
        for odd, cells in enumerate((low + high, low - high)):
            cells = cells.reshape(LANES, 2 * LANES)
            left = jnp.dot(outers[odd], cells[:, :LANES], preferred_element_type=wide)
            right = jnp.dot(outer_ref[odd], cells[:, LANES:], preferred_element_type=wide)
            for wave in range(WAVES):
                rows = pl.ds(SLABS * wave + step * odd, step)
                twist(left, SLABS * wave, odd, za_ref.at[group], rows)
                twist(right, SLABS * wave, odd, zb_ref.at[group], rows)
            twist(left, SLABS * WAVES, odd, ze_ref, pl.ds(SLABS * group + step * odd, step))
        if group:
            right_cells(group - 1)
    right_cells(GROUPS - 1)

    quarter = lax.broadcasted_iota(jnp.int32, (16, 128), 1) // SLABS
    changes = [jnp.where(quarter == 0, turned(shift_ref[...], -fine), 0.0) for fine in range(4)]
    changes = [jnp.concatenate([change] * 2, axis=0) for change in changes]
    weights = [jnp.concatenate([weight_ref[fine]] * 2, axis=0) for fine in range(4)]
    for pair in range(2):
        apart = lax.dot_general(inner, ze_ref[pair], NT, preferred_element_type=wide)
        for group in range(GROUPS):
            own = pl.ds(64 * group + 32 * pair, 32)
            value = lax.dot_general(inner, za_ref[group, pair], NT, preferred_element_type=wide)
            moved = turned(apart, -group)
            for part in range(2):
                for fine in range(4):
                    rows = slice(128 * part + 32 * fine, 128 * part + 32 * (fine + 1))
                    scaled = value[rows] * weights[fine]
                    changed = scaled[:, :128] + moved[rows] * changes[fine]
                    a_ref[part, fine, own, :128] = changed.astype(jnp.bfloat16)
                    a_ref[part, fine, own, 128:] = scaled[:, 128:].astype(jnp.bfloat16)

    product = jnp.zeros((LANES, LANES), wide)
    for part in range(2):
        for fine in range(4):
            product += lax.dot_general(a_ref[part, fine], b_ref[part, fine], NT, preferred_element_type=wide)
    below = lax.broadcasted_iota(jnp.int32, (LANES, LANES), 0)
    along = lax.broadcasted_iota(jnp.int32, (LANES, LANES), 1)
    product = jnp.where(below % 16 == along % 16, product, 0.0)
    rows = jnp.concatenate([product[16 * k : 16 * (k + 1)].sum(0, keepdims=True) for k in range(16)], axis=0)
    below, along = (lax.broadcasted_iota(jnp.int32, (LANES, 128), axis) for axis in range(2))
    gather = jnp.where(below // 16 == along % 16, 1.0, 0.0).astype(jnp.bfloat16)
    total = jnp.zeros((16, 128), wide)
    for _ in range(3):
        piece = rows.astype(jnp.bfloat16)
        rows = rows - piece.astype(wide)
        total += jnp.dot(piece, gather, preferred_element_type=wide)
    below, along = (lax.broadcasted_iota(jnp.int32, (16, 128), axis) for axis in range(2))
    total = jnp.where(below % ROWS == along // 16, total, 0.0)
    sums = [total[ROWS * group : ROWS * (group + 1)].sum(0, keepdims=True) for group in range(GROUPS)]
    for slab in range(SLABS):
        for group in range(GROUPS):
            out_ref[group * SLABS + slab] = sums[group]


def cross_partial(arrived, outer, twist, inner, weight, shift):
    return pl.pallas_call(
        cross_kernel,
        in_specs=[pl.BlockSpec(memory_space=pltpu.VMEM)] * 6,
        out_specs=pl.BlockSpec(memory_space=pltpu.VMEM),
        out_shape=jax.ShapeDtypeStruct((SLABS * GROUPS, 1, 128), jnp.float32),
        scratch_shapes=[
            pltpu.VMEM((GROUPS, 2, LANES, LANES), jnp.bfloat16),
            pltpu.VMEM((GROUPS, 2, LANES, LANES), jnp.bfloat16),
            pltpu.VMEM((2, 128, LANES), jnp.bfloat16),
            pltpu.VMEM((2, 4, LANES, LANES), jnp.bfloat16),
            pltpu.VMEM((2, 4, LANES, LANES), jnp.bfloat16),
        ],
        compiler_params=pltpu.CompilerParams(vmem_limit_bytes=36 * 2**20),
        cost_estimate=pl.CostEstimate(flops=3 * 10**9, bytes_accessed=5 * 2**20, transcendentals=0),
    )(arrived, outer, twist, inner, weight, shift)


def lookup(indices, table):
    onehot = indices[:, None] == jnp.arange(table.shape[0], dtype=jnp.int32)[None, :]
    return jnp.sum(jnp.where(onehot, table[None, :], 0.0), axis=1)


def shards(first_block, second_block, spectrum, first_ids, second_ids, error_scale):
    half, outer, twist, inner = (jnp.asarray(t) for t in make_tables())
    sent = half_transform(first_block.reshape(LANES, N), second_block.reshape(LANES, N), half)
    sent = sent.reshape(SLABS * GROUPS, 16, 2 * LANES)
    arrived = lax.all_to_all(sent, EVERY, 0, 0, tiled=True)
    nyquist = lax.ppermute(spectrum[:1], "grid", [(SLABS // 2, 0)])
    weight, shift = spectrum_weights(spectrum, nyquist)
    arrived = arrived.reshape(GROUPS, SLABS, 16, 2 * LANES)
    partial = cross_partial(arrived, outer, twist, inner, weight, shift)
    factor = 1.0 / (N * lookup(first_ids, error_scale)[:, None] * lookup(second_ids, error_scale)[None, :])
    partial, factor = lax.optimization_barrier((partial, factor))
    partial = lax.all_to_all(partial, EVERY, 0, 0, tiled=True)
    return partial.sum((0, 1))[:64].reshape(ROWS, GROUPS * ROWS) * factor


def solution(mesh):
    return jax.shard_map(
        shards,
        mesh=mesh,
        in_specs=(
            P("row", "grid", None),
            P("row", "grid", None),
            P("grid", None),
            P("row"),
            P(),
            P(),
        ),
        out_specs=P("row", None),
        check_vma=False,
    )
```
